128 devices in a mesh: batch: 16 (over z, y), tp: 8 (over x, core).
Axes of the slice: x: 4, y: 4, z: 4, core: 2. Of those that a mesh axis runs over, the one named last changes fastest.
Arguments:
- tokens: bfloat16 [1024, 6144], P('batch', 'tp'), may hold values from -6 to 6
- queries: bfloat16 [1024, 48, 128], P('batch', 'tp'), may hold values from -6 to 6
- new_keys: bfloat16 [1024, 8, 128], P('batch', 'tp'), may hold values from -6 to 6
- new_values: bfloat16 [1024, 8, 128], P('batch', 'tp'), may hold values from -16 to 16
- key_cache: bfloat16 [1024, 8, 128, 128], P('batch', 'tp'), may hold values from -6 to 6
- value_cache: bfloat16 [1024, 8, 128, 128], P('batch', 'tp'), may hold values from -16 to 16
- lengths: int32 [1024], P('batch'), may hold values from 1 to 128, 65536 in all
- routes: int32 [1024, 2], P('batch'), may hold values from 0 to 3, all different within a row; in each aligned block of 64 rows (0 to 63, 64 to 127, ...) at most 40 rows name the same one
- out_weight: bfloat16 [6144, 6144], P('tp'), may hold values from -0.078125 to 0.078125
- norm_gain: bfloat16 [6144], replicated, may hold values from 0.099609375 to 1.8984375
- router: float32 [6144, 4], replicated, may hold values from -0.078125 to 0.078125
- gate_weight: bfloat16 [6144, 32768], P(None, ('batch', 'tp')), may hold values from -0.078125 to 0.078125
- up_weight: bfloat16 [6144, 32768], P(None, ('batch', 'tp')), may hold values from -0.078125 to 0.078125
- down_weight: bfloat16 [32768, 6144], P(('batch', 'tp')), may hold values from -0.0625 to 0.0625
Outputs:
- mixed: bfloat16 [1024, 6144], P('batch', 'tp')
The draws below stay inside these ranges and needn't reach their ends.
Inputs may be any that keep to these rules, and one draw needn't show every extreme that they name: `routes`: the two experts of a token differ. In each aligned block of 64 rows (the rows of one batch index) no expert is named by more than 40 rows, a bound that some block reaches.
All inputs are finite; a program needn't handle non-finite values. No bound on the sum of `lengths` on one device may be relied on, other than what follows from the above.
Results may differ from the reference program's by a relative error of at most 0.024.
Values may be sent and summed in bfloat16 or wider, within the bound.
No kernel may reach another device: no remote copies, remote signals or barrier semaphores. Data moves between devices by JAX's collectives and lax.ppermute only.
A program may use at most 128 MiB of HBM per device.

```python
import math
import jax
import jax.numpy as jnp
import numpy as np
from jax import lax

D = 6144
HEADS = 48
KV_HEADS = 8
HEAD_DIM = 128
EXPERTS = 4
FF = 8192
TOK_DEV = 64
LMAX = 128
TOKENS = 1024
CAP = 40
FF_DEV = 256


def base_keys(key):
    return jnp.clip(jax.random.normal(jax.random.fold_in(key, 101), (TOKENS, KV_HEADS, HEAD_DIM), jnp.float32), -6.0, 6.0)


def draw_new_keys(key, part):
    base = base_keys(key)
    return base.astype(jnp.bfloat16)


def draw_queries(key, part):
    key = jax.random.fold_in(key, 2)
    drawn = jnp.clip(jax.random.normal(key, (TOKENS, HEADS, HEAD_DIM), jnp.float32), -6.0, 6.0)
    return drawn.astype(jnp.bfloat16)


def draw_key_cache(key, part):
    key = jax.random.fold_in(key, 3)
    cache = jnp.clip(jax.random.normal(key, (TOKENS, KV_HEADS, LMAX, HEAD_DIM), jnp.float32), -6.0, 6.0)
    return cache.astype(jnp.bfloat16)


def level_of(key, extent, split, low, largest):
    level = 1.0
    for axis_at, blocks in split:
        draws = jax.random.uniform(jax.random.fold_in(jax.random.fold_in(key, 6), axis_at), (blocks,), jnp.float32, low / len(split), largest / len(split))
        level = level * jnp.repeat(jnp.exp(draws), extent[axis_at] // blocks).reshape((-1,) + (1,) * (len(extent) - 1 - axis_at))
    return level


def split_up(number_of, total, limit, lean):
    portions = [(1 << 20) // math.isqrt(standing ** lean) + 1 for standing in range(2, number_of + 1)]
    surplus, counts = total - limit - (number_of - 1), [1] * (number_of - 1)
    while surplus > 0:
        free = [i for i in range(number_of - 1) if counts[i] < limit]
        mass, remaining = sum([portions[i] for i in free]), surplus
        for i in free:
            extra = min(limit - counts[i], max(1, remaining * portions[i] // mass), surplus)
            counts[i] = counts[i] + extra
            surplus = surplus - extra
    return np.array([limit] + counts)


def ragged_sizes(rng, amount, total, reach, lean):
    if amount == 2:
        one = jax.random.randint(rng, (), max(1, total - reach), min(reach, total - 1) + 1)
        return jnp.stack([one, total - one])
    tallies = jnp.asarray(split_up(amount, total, reach, lean), jnp.int32)
    pairs = (amount - 1) // 2
    source_of, taker = tallies[1:1 + 2 * pairs:2], tallies[2:2 + 2 * pairs:2]
    room = jnp.minimum(source_of - 1, reach - taker)
    moved = jax.random.randint(jax.random.fold_in(rng, 1), (pairs,), 0, 1 << 20) % (room + 1)
    tallies = tallies.at[1:1 + 2 * pairs:2].set(source_of - moved).at[2:2 + 2 * pairs:2].set(taker + moved)
    return tallies[jax.random.permutation(jax.random.fold_in(rng, 2), amount)]


def routed_block(own_key, own, number, rows, amount, top, reach, slope):
    order = jax.random.permutation(own_key, amount)
    heavy_load, usual = load_shares(amount, rows * top, reach, slope, True), load_shares(amount, rows * top, reach, slope, False)
    places = jnp.arange(amount)

    def named(sizes, rotation):
        used = int((sizes > 0).sum())
        fixed = max(1, used // 4)
        moved = fixed + (places - fixed + rotation * (used - fixed)) % max(1, amount - fixed)
        return jnp.zeros((amount,), jnp.int32).at[order[jnp.where(places < fixed, places, moved)]].set(jnp.asarray(sizes, jnp.int32))

    sizes = jnp.where(number % 4 == 0, named(heavy_load, number // 4), named(usual, number - number // 4 - 1))
    mixed = jax.random.permutation(jax.random.fold_in(own, 3), amount)
    giver, receiver = mixed[0:amount // 2 * 2:2], mixed[1:amount // 2 * 2:2]
    room = jnp.minimum(sizes[giver] - 1, reach - sizes[receiver]) // 2
    room = jnp.where((giver == order[0]) | (receiver == order[0]) | (sizes[receiver] == 0), 0, jnp.maximum(room, 0))
    moved = jax.random.randint(jax.random.fold_in(own, 4), (amount // 2,), 0, 1 << 20) % (room + 1)
    sizes = sizes.at[giver].add(-moved).at[receiver].add(moved)
    items = jnp.searchsorted(jnp.cumsum(sizes), jnp.arange(rows * top), side="right").astype(jnp.int32)
    grid = items.reshape(top, rows).T
    grid = grid[jax.random.permutation(jax.random.fold_in(own, 1), rows)]
    rotation = jax.random.randint(jax.random.fold_in(own, 2), (rows, 1), 0, top)
    return jnp.take_along_axis(grid, (jnp.arange(top)[None, :] + rotation) % top, axis=1)


def load_shares(number_of, total, bound, skew, full):
    weights = [(1 << 20) // math.isqrt(standing ** skew) + 1 for standing in range(1, number_of + 1)]
    largest = bound if full else min(bound, max(-(-total // number_of), total * weights[0] // sum(weights)))
    least = 1 if total - largest >= number_of - 1 else 0
    counts, surplus = [largest] + [least] * (number_of - 1), total - largest - least * (number_of - 1)
    while surplus > 0:
        movable = [i for i in range(1, number_of) if counts[i] < largest] or [i for i in range(1, number_of) if counts[i] < bound]
        mass, left = sum([weights[i] for i in movable]), surplus
        for i in movable:
            addition = min(bound - counts[i], max(1, left * weights[i] // mass), surplus)
            counts[i] = counts[i] + addition
            surplus = surplus - addition
    return np.array(counts)


def gaussian(rng, dims, scale, most, shards=(), kind=jnp.bfloat16):
    level = level_of(rng, dims, shards, -0.22, 0.18) if shards else 1.0
    entries = jax.random.normal(rng, dims, jnp.float32) * scale * level
    return jnp.minimum(jnp.maximum(entries, -most), most).astype(kind)


def setup_inputs(seed: int = 0) -> dict:
    key_list = jax.random.split(jax.random.key(seed), 15)
    tokens = gaussian(key_list[0], (TOKENS, D), 1.0, 6.0, ((0, 16), (1, 8)))
    queries = draw_queries(jax.random.fold_in(key_list[14], 71), 0)
    new_keys = draw_new_keys(jax.random.fold_in(key_list[14], 71), 0)
    new_values = gaussian(key_list[3], (TOKENS, KV_HEADS, HEAD_DIM), 4.0, 16.0, ((0, 16), (1, 8)))
    key_cache = draw_key_cache(jax.random.fold_in(key_list[14], 71), 0)
    value_cache = gaussian(key_list[5], (TOKENS, KV_HEADS, LMAX, HEAD_DIM), 4.0, 16.0, ((0, 16), (1, 8)))
    lengths = ragged_sizes(key_list[6], TOKENS, TOKENS * LMAX // 2, LMAX, 2).astype(jnp.int32)
    routes_keys = jax.random.split(jax.random.fold_in(key_list[7], 1), TOKENS // TOK_DEV)
    routes_turns = jax.random.permutation(jax.random.fold_in(key_list[7], 3), TOKENS // TOK_DEV)
    routes = jax.vmap(lambda own, number: routed_block(jax.random.fold_in(key_list[7], 2), own, number, TOK_DEV, EXPERTS, 2, CAP, 2))(routes_keys, routes_turns).reshape((TOKENS, 2))
    out_weight = gaussian(key_list[8], (HEADS * HEAD_DIM, D), (HEADS * HEAD_DIM) ** -0.5, 0.078125, ((0, 8),))
    norm_gain = jnp.clip(1.0 + 0.18 * jax.random.normal(key_list[9], (D,), jnp.float32), 0.099609375, 1.8984375).astype(jnp.bfloat16)
    router = gaussian(key_list[10], (D, EXPERTS), D ** -0.5, 0.078125, (), jnp.float32)
    gate_weight = gaussian(key_list[11], (D, EXPERTS * FF), D ** -0.5, 0.078125, ((1, 128),))
    up_weight = gaussian(key_list[12], (D, EXPERTS * FF), D ** -0.5, 0.078125, ((1, 128),))
    down_weight = gaussian(key_list[13], (EXPERTS * FF, D), FF ** -0.5, 0.0625, ((0, 128),))
    return dict(tokens=tokens, queries=queries, new_keys=new_keys, new_values=new_values, key_cache=key_cache, value_cache=value_cache, lengths=lengths, routes=routes, out_weight=out_weight, norm_gain=norm_gain, router=router, gate_weight=gate_weight, up_weight=up_weight, down_weight=down_weight)


EPS = 1e-05

def attend(queries, new_keys, new_values, key_cache, value_cache, lengths):
    groups = HEADS // KV_HEADS
    grouped = queries.astype(jnp.float32).reshape(TOKENS, KV_HEADS, groups, HEAD_DIM)
    scale = 1.0 / math.sqrt(HEAD_DIM)
    scores = jnp.einsum('tgqd,tgld->tgql', grouped, key_cache.astype(jnp.float32)) * scale
    own = jnp.einsum('tgqd,tgd->tgq', grouped, new_keys.astype(jnp.float32)) * scale
    position = jnp.arange(LMAX, dtype=jnp.int32)
    valid = position[None, None, None, :] < lengths[:, None, None, None]
    masked = jnp.where(valid, scores, -jnp.inf)
    top = jnp.maximum(lax.optimization_barrier(jnp.max(masked, axis=-1)), own)
    weights = jnp.where(valid, jnp.exp(scores - top[..., None]), 0.0)
    own_weight = jnp.exp(own - top)
    total = lax.optimization_barrier(jnp.sum(weights, axis=-1)) + own_weight
    probs = (weights / total[..., None]).astype(jnp.bfloat16)
    own_prob = (own_weight / total).astype(jnp.bfloat16)
    context = jnp.einsum('tgql,tgld->tgqd', probs.astype(jnp.float32), value_cache.astype(jnp.float32))
    context = context + own_prob.astype(jnp.float32)[..., None] * new_values.astype(jnp.float32)[:, :, None, :]
    return context.astype(jnp.bfloat16).reshape(TOKENS, HEADS * HEAD_DIM)

def expert_output(normed, gate_block, up_block, down_block):
    gate = jnp.dot(normed, gate_block, preferred_element_type=jnp.float32)
    upper = jnp.dot(normed, up_block, preferred_element_type=jnp.float32)
    activation = (jax.nn.silu(gate) * upper).astype(jnp.bfloat16)
    blocks = FF // FF_DEV
    pieces = jnp.moveaxis(activation.reshape(TOKENS, blocks, FF_DEV), 1, 0)
    down_pieces = down_block.reshape(blocks, FF_DEV, D)

    def add_block(total, inputs):
        piece, down_piece = inputs
        term = lax.optimization_barrier(jnp.dot(piece, down_piece, preferred_element_type=jnp.float32).astype(jnp.bfloat16))
        return (total + term.astype(jnp.float32), None)
    result, _ = lax.scan(add_block, jnp.zeros((TOKENS, D), jnp.float32), (pieces, down_pieces))
    return result

def reference(tokens, queries, new_keys, new_values, key_cache, value_cache, lengths, routes, out_weight, norm_gain, router, gate_weight, up_weight, down_weight):
    context = attend(queries, new_keys, new_values, key_cache, value_cache, lengths)
    hidden_state = tokens.astype(jnp.float32) + jnp.dot(context, out_weight, preferred_element_type=jnp.float32)
    inverse_rms = lax.rsqrt(lax.optimization_barrier(jnp.mean(hidden_state * hidden_state, axis=-1, keepdims=True)) + EPS)
    scaled = hidden_state * inverse_rms * norm_gain.astype(jnp.float32)
    normed = scaled.astype(jnp.bfloat16)
    logits = jnp.dot(scaled, router, precision=lax.Precision.HIGHEST)
    chosen = jnp.take_along_axis(logits, routes, axis=1)
    first_weight = jax.nn.sigmoid(chosen[:, 0] - chosen[:, 1])
    second_weight = 1.0 - first_weight
    mixture = jnp.zeros((TOKENS, D), jnp.float32)
    for expert in range(EXPERTS):
        weight_e = jnp.where(routes[:, 0] == expert, first_weight, 0.0) + jnp.where(routes[:, 1] == expert, second_weight, 0.0)
        output_e = expert_output(normed, gate_weight[:, expert * FF:(expert + 1) * FF], up_weight[:, expert * FF:(expert + 1) * FF], down_weight[expert * FF:(expert + 1) * FF])
        mixture = mixture + weight_e[:, None] * output_e
    return (hidden_state + mixture).astype(jnp.bfloat16)
```

```python
import functools
import math

import jax
import jax.numpy as jnp
from jax import lax
from jax.experimental import pallas as pl
from jax.experimental.pallas import tpu as pltpu
from jax.sharding import Mesh
from jax.sharding import PartitionSpec as P

CAP = 40
EPS = 1e-05
D = 6144
BLK = 768
ROWS = 160
HID = 256
OFFS = (0, 1, -1, 2)
AXES = ("z", "y", "x", "c")
VMEM = pl.BlockSpec(memory_space=pltpu.VMEM)
SMEM = pl.BlockSpec(memory_space=pltpu.SMEM)
LIMIT = 56 * 1024 * 1024


def device_index(z, y, x, c):
    return ((z * 4 + y) * 4 + x) * 2 + c


def second_pairs(shift):
    pairs = []
    for z in range(4):
        for y in range(4):
            for x in range(4):
                pairs.append((device_index(z, y, x, 0), device_index(z, (y + shift) % 4, x, 0)))
                pairs.append((device_index(z, y, x, 1), device_index(z, y, (x + shift) % 4, 1)))
    return pairs


def first_groups():
    four = range(4)
    groups = [[device_index(z, y, x, 0) for x in four for z in four] for y in four]
    groups += [[device_index(z, y, x, 1) for y in four for z in four] for x in four]
    return groups


def along_second(a, shift):
    return lax.ppermute(a, AXES, second_pairs(shift))


def along_first(a):
    return lax.all_to_all(a, AXES, 0, 0, tiled=True, axis_index_groups=first_groups())


def along_x(a, shift):
    return lax.ppermute(a, "x", [(i, (i + shift) % 4) for i in range(4)])


def swap_cores(a):
    return lax.ppermute(a, "c", [(0, 1), (1, 0)])


def attend_local(queries, new_keys, new_values, key_cache, value_cache, lengths):
    row_count, head_count, head_size = queries.shape
    kv_local = new_keys.shape[1]
    cache_len = key_cache.shape[2]
    grouped = queries.reshape(row_count, kv_local, head_count // kv_local, head_size)
    scale = 1.0 / math.sqrt(head_size)
    scores = (
        jnp.einsum("tgqd,tgld->tgql", grouped, key_cache, preferred_element_type=jnp.float32)
        * scale
    )
    own = jnp.einsum("tgqd,tgd->tgq", grouped, new_keys, preferred_element_type=jnp.float32) * scale
    position = jnp.arange(cache_len, dtype=jnp.int32)
    valid = position[None, None, None, :] < lengths[:, None, None, None]
    masked = jnp.where(valid, scores, -jnp.inf)
    top = jnp.maximum(jnp.max(masked, axis=-1), own)
    weights = jnp.where(valid, jnp.exp(scores - top[..., None]), 0.0)
    own_weight = jnp.exp(own - top)
    total = jnp.sum(weights, axis=-1) + own_weight
    probs = (weights / total[..., None]).astype(jnp.bfloat16)
    own_prob = (own_weight / total).astype(jnp.bfloat16)
    context = jnp.einsum("tgql,tgld->tgqd", probs, value_cache, preferred_element_type=jnp.float32)
    context = (
        context
        + own_prob.astype(jnp.float32)[..., None] * new_values.astype(jnp.float32)[:, :, None, :]
    )
    return context.astype(jnp.bfloat16).reshape(row_count, head_count * head_size)


def project_kernel(half_ref, context_ref, weight_ref, out_ref):
    out_ref[0] = jnp.dot(
        context_ref[...], weight_ref[...], preferred_element_type=jnp.float32
    ).astype(out_ref.dtype)


def project(half, context, out_weight, dtype):
    rows = context.shape[0]
    return pl.pallas_call(
        project_kernel,
        out_shape=jax.ShapeDtypeStruct((4, rows, BLK), dtype),
        grid_spec=pltpu.PrefetchScalarGridSpec(
            num_scalar_prefetch=1,
            grid=(4,),
            in_specs=[
                pl.BlockSpec((rows, BLK), lambda i, half: (0, 0)),
                pl.BlockSpec((BLK, BLK), lambda i, half: (0, 2 * i + half[0])),
            ],
            out_specs=pl.BlockSpec((1, rows, BLK), lambda i, half: (i, 0, 0)),
        ),
        compiler_params=pltpu.CompilerParams(vmem_limit_bytes=LIMIT),
        cost_estimate=pl.CostEstimate(
            flops=2 * rows * BLK * BLK * 4, bytes_accessed=BLK * BLK * 8, transcendentals=0
        ),
    )(half, context, out_weight)


def block_rows(index):
    return pl.ds(pl.multiple_of(index * BLK, BLK), BLK)


def line_rows(index):
    return pl.ds(pl.multiple_of(index * ROWS, ROWS), ROWS)


def enter_kernel(place, g0, g1, g2, g3, gate, up, gate_far, up_far, inverse, mine, far):
    x, y, c = place[0], place[1], place[2]
    pieces = (g0, g1, g2, g3)

    def squares(piece, block):
        value = piece.astype(jnp.float32) * inverse[pl.ds(block, 1), :]
        value = value * value
        total = value[:, :128]
        for i in range(1, BLK // 128):
            total += value[:, i * 128 : (i + 1) * 128]
        return total

    def dot(a, b):
        return jnp.dot(a, b, preferred_element_type=jnp.float32)

    @pl.when(c == 0)
    def _():
        for j, shift in enumerate(OFFS):
            rows = line_rows((y - shift + 4) % 4)
            parts = None
            for k in range(4):
                block = 2 * k
                piece = pieces[j][k * ROWS : (k + 1) * ROWS, :]
                terms = [
                    dot(piece, gate[block * BLK : (block + 1) * BLK, :]),
                    dot(piece, up[block * BLK : (block + 1) * BLK, :]),
                    dot(piece, gate_far[k * BLK : (k + 1) * BLK, :]),
                    dot(piece, up_far[k * BLK : (k + 1) * BLK, :]),
                    squares(piece, block),
                ]
                parts = terms if parts is None else [a + b for a, b in zip(parts, terms)]
            mine[rows, :HID] = parts[0]
            mine[rows, HID : 2 * HID] = parts[1]
            mine[rows, 2 * HID :] = parts[4]
            far[rows, :HID] = parts[2]
            far[rows, HID : 2 * HID] = parts[3]
            far[rows, 2 * HID :] = parts[4]

    @pl.when(c == 1)
    def _():
        for j, shift in enumerate(OFFS):
            k = (x - shift + 4) % 4
            block = 2 * k + 1

            def step(r, carry, j=j, k=k, block=block):
                rows = line_rows(r)
                piece = pieces[j][rows, :]
                square = squares(piece, block)
                terms = [
                    dot(piece, gate[block_rows(block), :]),
                    dot(piece, up[block_rows(block), :]),
                    square,
                    dot(piece, gate_far[block_rows(k), :]),
                    dot(piece, up_far[block_rows(k), :]),
                    square,
                ]
                spots = (slice(0, HID), slice(HID, 2 * HID), slice(2 * HID, None))
                for n, term in enumerate(terms):
                    ref = mine if n < 3 else far
                    if j == 0:
                        ref[rows, spots[n % 3]] = term
                    else:
                        ref[rows, spots[n % 3]] += term
                return carry

            lax.fori_loop(0, 4, step, 0)


def enter(place, pieces, gate, up, gate_far, up_far, inverse):
    shape = jax.ShapeDtypeStruct((4 * ROWS, 2 * HID + 128), jnp.float32)
    return pl.pallas_call(
        enter_kernel,
        out_shape=(shape, shape),
        in_specs=[SMEM] + [VMEM] * 9,
        out_specs=(VMEM, VMEM),
        compiler_params=pltpu.CompilerParams(vmem_limit_bytes=LIMIT),
        cost_estimate=pl.CostEstimate(
            flops=2 * 4 * ROWS * 4 * BLK * 4 * HID, bytes_accessed=4000000, transcendentals=0
        ),
    )(place, *pieces, gate, up, gate_far, up_far, inverse)


def activate_kernel(mine, far, out):
    for r in range(4):
        rows = slice(r * ROWS, (r + 1) * ROWS)
        total = mine[rows, :] + far[rows, :]
        mean = jnp.sum(total[:, 2 * HID :], axis=1, keepdims=True) * (1.0 / D)
        scale = lax.rsqrt(mean + EPS)
        gate = total[:, :HID] * scale
        upper = total[:, HID : 2 * HID] * scale
        out[rows, :] = (gate * (1.0 / (1.0 + jnp.exp(-gate))) * upper).astype(jnp.bfloat16)


def activate(mine, far):
    return pl.pallas_call(
        activate_kernel,
        out_shape=jax.ShapeDtypeStruct((4 * ROWS, HID), jnp.bfloat16),
        in_specs=[VMEM] * 2,
        out_specs=VMEM,
        compiler_params=pltpu.CompilerParams(vmem_limit_bytes=LIMIT),
    )(mine, far)


def leave_kernel(place, act, act_far, down, down_far, o0, o1, o2, o3):
    x, y, c = place[0], place[1], place[2]
    outs = (o0, o1, o2, o3)

    def dot(a, b):
        return jnp.dot(a, b, preferred_element_type=jnp.float32)

    @pl.when(c == 0)
    def _():
        for j, shift in enumerate(OFFS):
            rows = line_rows((y + shift + 4) % 4)
            for k in range(4):
                term = dot(act[rows, :], down[:, 2 * k * BLK : (2 * k + 1) * BLK])
                term += dot(act_far[rows, :], down_far[:, k * BLK : (k + 1) * BLK])
                outs[j][k * ROWS : (k + 1) * ROWS, :] = term.astype(jnp.bfloat16)

    @pl.when(c == 1)
    def _():
        for j, shift in enumerate(OFFS):
            k = (x + shift + 4) % 4

            def step(r, carry, j=j, k=k):
                rows = line_rows(r)
                term = dot(act[rows, :], down[:, block_rows(2 * k + 1)])
                term += dot(act_far[rows, :], down_far[:, block_rows(k)])
                outs[j][rows, :] = term.astype(jnp.bfloat16)
                return carry

            lax.fori_loop(0, 4, step, 0)


def leave(place, act, act_far, down, down_far):
    shape = jax.ShapeDtypeStruct((4 * ROWS, BLK), jnp.bfloat16)
    return pl.pallas_call(
        leave_kernel,
        out_shape=(shape,) * 4,
        in_specs=[SMEM] + [VMEM] * 4,
        out_specs=(VMEM,) * 4,
        compiler_params=pltpu.CompilerParams(vmem_limit_bytes=LIMIT),
        cost_estimate=pl.CostEstimate(
            flops=2 * 4 * ROWS * 4 * BLK * 2 * HID, bytes_accessed=4000000, transcendentals=0
        ),
    )(place, act, act_far, down, down_far)


def slots(routes, expert_count):
    row_count = routes.shape[0]
    expert_ids = jnp.arange(expert_count, dtype=jnp.int32)
    picked = routes[:, :, None] == expert_ids[None, None, :]
    flat = picked.reshape(row_count * 2, expert_count).astype(jnp.int32)
    ranks = (jnp.cumsum(flat, axis=0) - flat).reshape(row_count, 2, expert_count)
    slot_index = jnp.sum(jnp.where(picked, ranks, 0), axis=-1)
    slot_hit = slot_index[:, :, None] == jnp.arange(CAP, dtype=jnp.int32)[None, None, :]
    return picked, picked[:, :, :, None] & slot_hit[:, :, None, :]


def shards(
    tokens,
    queries,
    new_keys,
    new_values,
    key_cache,
    value_cache,
    lengths,
    routes,
    out_weight,
    norm_gain,
    router,
    gate_weight,
    up_weight,
    down_weight,
):
    row_count = tokens.shape[0]
    expert_count = router.shape[1]
    x, y, c = lax.axis_index("x"), lax.axis_index("y"), lax.axis_index("c")
    place = jnp.stack([x, y, c]).astype(jnp.int32)
    here = 2 * x + c

    def other_half(weight):
        return lax.dynamic_index_in_dim(weight.reshape(4, 2, BLK, HID), 1 - c, 1, keepdims=False)

    gate_far = swap_cores(other_half(gate_weight).reshape(4 * BLK, HID))
    up_far = swap_cores(other_half(up_weight).reshape(4 * BLK, HID))
    down_far = swap_cores(
        lax.dynamic_index_in_dim(
            down_weight.reshape(HID, 4, 2, BLK), 1 - c, 2, keepdims=False
        ).reshape(HID, 4 * BLK)
    )
    gain = norm_gain.astype(jnp.float32).reshape(8, BLK)
    inverse = 1.0 / gain

    context = attend_local(queries, new_keys, new_values, key_cache, value_cache, lengths)
    core = c.astype(jnp.int32)[None]
    for_other = project(1 - core, context, out_weight, jnp.bfloat16)
    from_other = swap_cores(for_other)
    terms = project(core, context, out_weight, jnp.float32) + from_other.astype(jnp.float32)

    def column(shift):
        return lax.dynamic_index_in_dim(terms, (x + shift + 4) % 4, 0, keepdims=False)

    hidden = column(0) + tokens.astype(jnp.float32)
    for shift in (2, 1, -1):
        hidden = hidden + along_x(column(shift).astype(jnp.bfloat16), shift).astype(jnp.float32)

    picked, matched = slots(routes, expert_count)
    scaled = hidden * lax.dynamic_index_in_dim(gain, here, 0)
    selection = jnp.any(matched, axis=1).astype(jnp.bfloat16)
    outgoing = jnp.einsum(
        "rec,rd->ecd", selection, scaled.astype(jnp.bfloat16), preferred_element_type=jnp.float32
    ).astype(jnp.bfloat16)
    outgoing = jnp.broadcast_to(outgoing[None], (4, 4, CAP, BLK)).reshape(16, CAP, BLK)
    line = along_first(outgoing).reshape(4 * ROWS, BLK)
    pieces = [line] + [along_second(line, shift) for shift in OFFS[1:]]

    own_router = lax.dynamic_slice_in_dim(router, here * BLK, BLK, 0)
    partial = jnp.concatenate(
        [
            jnp.dot(scaled, own_router, precision=lax.Precision.HIGHEST),
            jnp.sum(hidden * hidden, axis=1, keepdims=True),
        ],
        axis=1,
    )
    partial = jnp.pad(partial, ((0, 0), (0, 128 - partial.shape[1])))
    partial = partial + swap_cores(partial)
    stats = partial + along_x(partial, 1) + along_x(partial, -1) + along_x(partial, 2)
    inverse_rms = lax.rsqrt(stats[:, expert_count : expert_count + 1] * (1.0 / D) + EPS)
    logits = stats[:, :expert_count] * inverse_rms
    chosen = jnp.sum(jnp.where(picked, logits[:, None, :], 0.0), axis=-1)
    first_weight = jax.nn.sigmoid(chosen[:, 0] - chosen[:, 1])
    route_weights = jnp.stack([first_weight, 1.0 - first_weight], axis=1)
    weighted = jnp.sum(jnp.where(matched, route_weights[:, :, None, None], 0.0), axis=1)

    mine, far = enter(place, pieces, gate_weight, up_weight, gate_far, up_far, inverse)
    act = activate(mine, swap_cores(far))
    outs = leave(place, act, swap_cores(act), down_weight, down_far)
    total = outs[0].astype(jnp.float32)
    for out, shift in zip(outs[1:], OFFS[1:]):
        total = total + along_second(out, shift).astype(jnp.float32)
    returned = along_first(total.astype(jnp.bfloat16).reshape(16, CAP, BLK))
    arrived = jnp.sum(returned.reshape(4, 4, CAP, BLK).astype(jnp.float32), axis=0)
    mixture = jnp.einsum("rec,ecd->rd", weighted, arrived, precision=lax.Precision.HIGHEST)
    return (hidden + mixture).astype(jnp.bfloat16)


def solution(mesh):
    grid = Mesh(mesh.devices.reshape(4, 4, 4, 2), AXES)
    batch, tp = ("z", "y"), ("x", "c")
    return jax.shard_map(
        shards,
        mesh=grid,
        in_specs=(
            P(batch, tp),
            P(batch, tp, None),
            P(batch, tp, None),
            P(batch, tp, None),
            P(batch, tp, None, None),
            P(batch, tp, None, None),
            P(batch),
            P(batch, None),
            P(tp, None),
            P(),
            P(),
            P(None, (*batch, *tp)),
            P(None, (*batch, *tp)),
            P((*batch, *tp), None),
        ),
        out_specs=P(batch, tp),
        check_vma=False,
    )
```

```python
import functools
import math

import jax
import jax.numpy as jnp
from jax import lax
from jax.experimental import pallas as pl
from jax.experimental.pallas import tpu as pltpu
from jax.sharding import Mesh
from jax.sharding import PartitionSpec as P

CAP = 40
EPS = 1e-05
D = 6144
BLK = 768
ROWS = 160
HID = 256
OFFS = (0, 1, -1, 2)
AXES = ("z", "y", "x", "c")
VMEM = pl.BlockSpec(memory_space=pltpu.VMEM)
SMEM = pl.BlockSpec(memory_space=pltpu.SMEM)
LIMIT = 16 * 1024 * 1024


def device_index(z, y, x, c):
    return ((z * 4 + y) * 4 + x) * 2 + c


def second_pairs(shift):
    pairs = []
    for z in range(4):
        for y in range(4):
            for x in range(4):
                pairs.append((device_index(z, y, x, 0), device_index(z, (y + shift) % 4, x, 0)))
                pairs.append((device_index(z, y, x, 1), device_index(z, y, (x + shift) % 4, 1)))
    return pairs


def first_groups():
    four = range(4)
    groups = [[device_index(z, y, x, 0) for x in four for z in four] for y in four]
    groups += [[device_index(z, y, x, 1) for y in four for z in four] for x in four]
    return groups


def along_second(a, shift):
    return lax.ppermute(a, AXES, second_pairs(shift))


def along_first(a):
    return lax.all_to_all(a, AXES, 0, 0, tiled=True, axis_index_groups=first_groups())


def along_x(a, shift):
    return lax.ppermute(a, "x", [(i, (i + shift) % 4) for i in range(4)])


def swap_cores(a):
    return lax.ppermute(a, "c", [(0, 1), (1, 0)])


def attend_local(queries, new_keys, new_values, key_cache, value_cache, lengths):
    row_count, head_count, head_size = queries.shape
    kv_local = new_keys.shape[1]
    cache_len = key_cache.shape[2]
    grouped = queries.reshape(row_count, kv_local, head_count // kv_local, head_size)
    scale = 1.0 / math.sqrt(head_size)
    scores = (
        jnp.einsum("tgqd,tgld->tgql", grouped, key_cache, preferred_element_type=jnp.float32)
        * scale
    )
    own = jnp.einsum("tgqd,tgd->tgq", grouped, new_keys, preferred_element_type=jnp.float32) * scale
    position = jnp.arange(cache_len, dtype=jnp.int32)
    valid = position[None, None, None, :] < lengths[:, None, None, None]
    masked = jnp.where(valid, scores, -jnp.inf)
    top = jnp.maximum(jnp.max(masked, axis=-1), own)
    weights = jnp.where(valid, jnp.exp(scores - top[..., None]), 0.0)
    own_weight = jnp.exp(own - top)
    total = jnp.sum(weights, axis=-1) + own_weight
    probs = (weights / total[..., None]).astype(jnp.bfloat16)
    own_prob = (own_weight / total).astype(jnp.bfloat16)
    context = jnp.einsum("tgql,tgld->tgqd", probs, value_cache, preferred_element_type=jnp.float32)
    context = (
        context
        + own_prob.astype(jnp.float32)[..., None] * new_values.astype(jnp.float32)[:, :, None, :]
    )
    return context.astype(jnp.bfloat16).reshape(row_count, head_count * head_size)


def near(a):
    return pltpu.with_memory_space_constraint(a, pltpu.VMEM)


def params():
    return pltpu.CompilerParams(vmem_limit_bytes=LIMIT)


def dot(a, b):
    return jnp.dot(a, b, preferred_element_type=jnp.float32)


def project_kernel(half, context, weight, out):
    for parity in range(2):

        @pl.when(half[0] == parity)
        def _():
            for i in range(4):
                start = (2 * i + parity) * BLK
                out[i] = dot(context[...], weight[:, start : start + BLK]).astype(out.dtype)


def project(half, context, out_weight, dtype):
    rows = context.shape[0]
    return pl.pallas_call(
        project_kernel,
        out_shape=pltpu.VMEM((4, rows, BLK), dtype),
        in_specs=[SMEM, VMEM, VMEM],
        out_specs=VMEM,
        compiler_params=params(),
        cost_estimate=pl.CostEstimate(
            flops=2 * rows * BLK * BLK * 4, bytes_accessed=BLK * BLK * 8, transcendentals=0
        ),
    )(half, near(context), near(out_weight))


def block_rows(index):
    return pl.ds(pl.multiple_of(index * BLK, BLK), BLK)


def line_rows(index):
    return pl.ds(pl.multiple_of(index * ROWS, ROWS), ROWS)


def squares(piece, inverse):
    value = piece.astype(jnp.float32) * inverse
    value = value * value
    total = value[:, :128]
    for i in range(1, BLK // 128):
        total += value[:, i * 128 : (i + 1) * 128]
    return total


def walk(place, pieces, emit):
    x, y, c = place[0], place[1], place[2]

    @pl.when(c == 0)
    def _():
        for j, shift in enumerate(OFFS):
            rows = line_rows((y - shift + 4) % 4)
            emit(rows, [(pieces[j][k * ROWS : (k + 1) * ROWS, :], k, 2 * k) for k in range(4)])

    @pl.when(c == 1)
    def _():
        blocks = [(x - shift + 4) % 4 for shift in OFFS]

        def step(r, carry):
            rows = line_rows(r)
            emit(rows, [(pieces[j][rows, :], k, 2 * k + 1) for j, k in enumerate(blocks)])
            return carry

        lax.fori_loop(0, 4, step, 0)


def total_of(terms):
    return functools.reduce(lambda a, b: a + b, terms)


def enter_far_kernel(place, g0, g1, g2, g3, gate, up, inverse, far, own):
    def emit(rows, parts):
        far[rows, :HID] = total_of([dot(p, gate[block_rows(k), :]) for p, k, _ in parts]).astype(far.dtype)
        far[rows, HID : 2 * HID] = total_of([dot(p, up[block_rows(k), :]) for p, k, _ in parts]).astype(far.dtype)
        square = total_of([squares(p, inverse[pl.ds(b, 1), :]) for p, _, b in parts])
        far[rows, 2 * HID :] = square.astype(far.dtype)
        own[rows, :] = square

    walk(place, (g0, g1, g2, g3), emit)


def enter_far(place, pieces, gate, up, inverse):
    return pl.pallas_call(
        enter_far_kernel,
        out_shape=(
            pltpu.VMEM((4 * ROWS, 2 * HID + 128), jnp.bfloat16),
            pltpu.VMEM((4 * ROWS, 128), jnp.float32),
        ),
        in_specs=[SMEM] + [VMEM] * 7,
        out_specs=(VMEM, VMEM),
        compiler_params=params(),
        cost_estimate=pl.CostEstimate(
            flops=2 * 4 * ROWS * 4 * BLK * 2 * HID, bytes_accessed=4000000, transcendentals=0
        ),
    )(place, *map(near, pieces), near(gate), near(up), near(inverse))


def enter_own_kernel(place, g0, g1, g2, g3, gate, up, own):
    def emit(rows, parts):
        own[rows, :HID] = total_of([dot(p, gate[block_rows(b), :]) for p, _, b in parts])
        own[rows, HID:] = total_of([dot(p, up[block_rows(b), :]) for p, _, b in parts])

    walk(place, (g0, g1, g2, g3), emit)


def enter_own(place, pieces, gate, up):
    return pl.pallas_call(
        enter_own_kernel,
        out_shape=pltpu.VMEM((4 * ROWS, 2 * HID), jnp.float32),
        in_specs=[SMEM] + [VMEM] * 6,
        out_specs=VMEM,
        compiler_params=params(),
        cost_estimate=pl.CostEstimate(
            flops=2 * 4 * ROWS * 4 * BLK * 2 * HID, bytes_accessed=4000000, transcendentals=0
        ),
    )(place, *map(near, pieces), near(gate), near(up))


def activate_kernel(own, square, far, out):
    for r in range(4):
        rows = slice(r * ROWS, (r + 1) * ROWS)
        other = far[rows, :].astype(jnp.float32)
        mean = jnp.sum(square[rows, :] + other[:, 2 * HID :], axis=1, keepdims=True) * (1.0 / D)
        scale = lax.rsqrt(mean + EPS)
        gate = (own[rows, :HID] + other[:, :HID]) * scale
        upper = (own[rows, HID:] + other[:, HID : 2 * HID]) * scale
        out[rows, :] = (gate * (1.0 / (1.0 + jnp.exp(-gate))) * upper).astype(jnp.bfloat16)


def activate(own, square, far):
    return pl.pallas_call(
        activate_kernel,
        out_shape=pltpu.VMEM((4 * ROWS, HID), jnp.bfloat16),
        in_specs=[VMEM] * 3,
        out_specs=VMEM,
        compiler_params=params(),
    )(near(own), near(square), near(far))


def leave_kernel(offsets, place, act, act_far, down, down_far, *outs):
    x, y, c = place[0], place[1], place[2]

    def term(rows, k):
        return (dot(act[rows, :], down[k]) + dot(act_far[rows, :], down_far[k])).astype(jnp.bfloat16)

    @pl.when(c == 0)
    def _():
        for out, shift in zip(outs, offsets):
            rows = line_rows((y + shift + 4) % 4)
            for k in range(4):
                out[k * ROWS : (k + 1) * ROWS, :] = term(rows, k)

    @pl.when(c == 1)
    def _():
        for out, shift in zip(outs, offsets):
            for r in range(4):
                rows = slice(r * ROWS, (r + 1) * ROWS)
                out[rows, :] = term(rows, (x + shift + 4) % 4)


def leave(offsets, place, act, act_far, down, down_far):
    return pl.pallas_call(
        functools.partial(leave_kernel, offsets),
        out_shape=(pltpu.VMEM((4 * ROWS, BLK), jnp.bfloat16),) * len(offsets),
        in_specs=[SMEM] + [VMEM] * 4,
        out_specs=(VMEM,) * len(offsets),
        compiler_params=params(),
        cost_estimate=pl.CostEstimate(
            flops=2 * 4 * ROWS * len(offsets) * BLK * 2 * HID, bytes_accessed=2000000, transcendentals=0
        ),
    )(place, near(act), near(act_far), near(down), near(down_far))


def slots(routes, expert_count):
    row_count = routes.shape[0]
    expert_ids = jnp.arange(expert_count, dtype=jnp.int32)
    picked = routes[:, :, None] == expert_ids[None, None, :]
    flat = picked.reshape(row_count * 2, expert_count).astype(jnp.int32)
    ranks = (jnp.cumsum(flat, axis=0) - flat).reshape(row_count, 2, expert_count)
    slot_index = jnp.sum(jnp.where(picked, ranks, 0), axis=-1)
    slot_hit = slot_index[:, :, None] == jnp.arange(CAP, dtype=jnp.int32)[None, None, :]
    return picked, picked[:, :, :, None] & slot_hit[:, :, None, :]


def shards(
    tokens,
    queries,
    new_keys,
    new_values,
    key_cache,
    value_cache,
    lengths,
    routes,
    out_weight,
    norm_gain,
    router,
    gate_weight,
    up_weight,
    down_weight,
):
    row_count = tokens.shape[0]
    expert_count = router.shape[1]
    x, y, c = lax.axis_index("x"), lax.axis_index("y"), lax.axis_index("c")
    place = jnp.stack([x, y, c]).astype(jnp.int32)
    here = 2 * x + c

    def other_half(weight):
        return lax.dynamic_index_in_dim(weight.reshape(4, 2, BLK, HID), 1 - c, 1, keepdims=False)

    gate_far = swap_cores(other_half(gate_weight).reshape(4 * BLK, HID))
    up_far = swap_cores(other_half(up_weight).reshape(4 * BLK, HID))

    def down_half(half):
        return jnp.stack(
            [lax.dynamic_slice_in_dim(down_weight, (2 * k + half) * BLK, BLK, 1) for k in range(4)]
        )

    down_own = down_half(c)
    down_far = swap_cores(down_half(1 - c))
    gain = norm_gain.astype(jnp.float32).reshape(8, BLK)
    inverse = 1.0 / gain

    context = attend_local(queries, new_keys, new_values, key_cache, value_cache, lengths)
    core = c.astype(jnp.int32)[None]
    for_other = project(1 - core, context, out_weight, jnp.bfloat16)
    from_other = swap_cores(for_other)
    terms = project(core, context, out_weight, jnp.float32) + from_other.astype(jnp.float32)

    def column(shift):
        return lax.dynamic_index_in_dim(terms, (x + shift + 4) % 4, 0, keepdims=False)

    hidden = column(0) + tokens.astype(jnp.float32)
    for shift in (2, 1, -1):
        hidden = hidden + along_x(column(shift).astype(jnp.bfloat16), shift).astype(jnp.float32)

    picked, matched = slots(routes, expert_count)
    scaled = hidden * lax.dynamic_index_in_dim(gain, here, 0)
    selection = jnp.any(matched, axis=1).astype(jnp.bfloat16)
    outgoing = jnp.einsum(
        "rec,rd->ecd", selection, scaled.astype(jnp.bfloat16), preferred_element_type=jnp.float32
    ).astype(jnp.bfloat16)
    outgoing = jnp.broadcast_to(outgoing[None], (4, 4, CAP, BLK)).reshape(16, CAP, BLK)
    line = along_first(outgoing).reshape(4 * ROWS, BLK)
    pieces = [line] + [along_second(line, shift) for shift in OFFS[1:]]

    own_router = lax.dynamic_slice_in_dim(router, here * BLK, BLK, 0)
    partial = jnp.concatenate(
        [
            jnp.dot(scaled, own_router, precision=lax.Precision.HIGHEST),
            jnp.sum(hidden * hidden, axis=1, keepdims=True),
        ],
        axis=1,
    )
    partial = jnp.pad(partial, ((0, 0), (0, 128 - partial.shape[1])))
    partial = partial + swap_cores(partial)
    stats = partial + along_x(partial, 1) + along_x(partial, -1) + along_x(partial, 2)
    inverse_rms = lax.rsqrt(stats[:, expert_count : expert_count + 1] * (1.0 / D) + EPS)
    logits = stats[:, :expert_count] * inverse_rms
    chosen = jnp.sum(jnp.where(picked, logits[:, None, :], 0.0), axis=-1)
    first_weight = jax.nn.sigmoid(chosen[:, 0] - chosen[:, 1])
    route_weights = jnp.stack([first_weight, 1.0 - first_weight], axis=1)
    weighted = jnp.sum(jnp.where(matched, route_weights[:, :, None, None], 0.0), axis=1)

    far, square = enter_far(place, pieces, gate_far, up_far, inverse)
    own = enter_own(place, pieces, gate_weight, up_weight)
    act = activate(own, square, swap_cores(far))
    act_far = swap_cores(act)
    (out2,) = leave((2,), place, act, act_far, down_own, down_far)
    out1, out3 = leave((1, -1), place, act, act_far, down_own, down_far)
    (out0,) = leave((0,), place, act, act_far, down_own, down_far)
    total = out0.astype(jnp.float32) + along_second(out2, 2).astype(jnp.float32)
    total = total + along_second(out1, 1).astype(jnp.float32)
    total = total + along_second(out3, -1).astype(jnp.float32)
    returned = along_first(total.astype(jnp.bfloat16).reshape(16, CAP, BLK))
    arrived = jnp.sum(returned.reshape(4, 4, CAP, BLK).astype(jnp.float32), axis=0)
    mixture = jnp.einsum("rec,ecd->rd", weighted, arrived, precision=lax.Precision.HIGHEST)
    return (hidden + mixture).astype(jnp.bfloat16)


def solution(mesh):
    grid = Mesh(mesh.devices.reshape(4, 4, 4, 2), AXES)
    batch, tp = ("z", "y"), ("x", "c")
    return jax.shard_map(
        shards,
        mesh=grid,
        in_specs=(
            P(batch, tp),
            P(batch, tp, None),
            P(batch, tp, None),
            P(batch, tp, None),
            P(batch, tp, None, None),
            P(batch, tp, None, None),
            P(batch),
            P(batch, None),
            P(tp, None),
            P(),
            P(),
            P(None, (*batch, *tp)),
            P(None, (*batch, *tp)),
            P((*batch, *tp), None),
        ),
        out_specs=P(batch, tp),
        check_vma=False,
    )
```

```python
import functools
import math

import jax
import jax.numpy as jnp
from jax import lax
from jax.experimental import pallas as pl
from jax.experimental.pallas import tpu as pltpu
from jax.sharding import Mesh
from jax.sharding import PartitionSpec as P

CAP = 40
EPS = 1e-05
D = 6144
BLK = 768
ROWS = 160
HID = 256
OFFS = (0, 1, -1, 2)
AXES = ("z", "y", "x", "c")
VMEM = pl.BlockSpec(memory_space=pltpu.VMEM)
SMEM = pl.BlockSpec(memory_space=pltpu.SMEM)
ANY = pl.BlockSpec(memory_space=pl.ANY)
LIMIT = 14 * 1024 * 1024


def device_index(z, y, x, c):
    return ((z * 4 + y) * 4 + x) * 2 + c


def plane_pairs(first, shift):
    pairs = []
    for z in range(4):
        for y in range(4):
            for x in range(4):
                for c in range(2):
                    if (c == 0) == first:
                        target = device_index(z, y, (x + shift) % 4, c)
                    else:
                        target = device_index(z, (y + shift) % 4, x, c)
                    pairs.append((device_index(z, y, x, c), target))
    return pairs


def along_first(a, shift):
    return lax.ppermute(a, AXES, plane_pairs(True, shift))


def along_second(a, shift):
    return lax.ppermute(a, AXES, plane_pairs(False, shift))


def along_z(a, shift):
    return lax.ppermute(a, "z", [(i, (i + shift) % 4) for i in range(4)])


def along_x(a, shift):
    return lax.ppermute(a, "x", [(i, (i + shift) % 4) for i in range(4)])


def swap_cores(a):
    return lax.ppermute(a, "c", [(0, 1), (1, 0)])


def attend_local(queries, new_keys, new_values, key_cache, value_cache, lengths):
    row_count, head_count, head_size = queries.shape
    kv_local = new_keys.shape[1]
    cache_len = key_cache.shape[2]
    grouped = queries.reshape(row_count, kv_local, head_count // kv_local, head_size)
    scale = 1.0 / math.sqrt(head_size)
    scores = (
        jnp.einsum("tgqd,tgld->tgql", grouped, key_cache, preferred_element_type=jnp.float32)
        * scale
    )
    own = jnp.einsum("tgqd,tgd->tgq", grouped, new_keys, preferred_element_type=jnp.float32) * scale
    position = jnp.arange(cache_len, dtype=jnp.int32)
    valid = position[None, None, None, :] < lengths[:, None, None, None]
    masked = jnp.where(valid, scores, -jnp.inf)
    top = jnp.maximum(jnp.max(masked, axis=-1), own)
    weights = jnp.where(valid, jnp.exp(scores - top[..., None]), 0.0)
    own_weight = jnp.exp(own - top)
    total = jnp.sum(weights, axis=-1) + own_weight
    probs = (weights / total[..., None]).astype(jnp.bfloat16)
    own_prob = (own_weight / total).astype(jnp.bfloat16)
    context = jnp.einsum("tgql,tgld->tgqd", probs, value_cache, preferred_element_type=jnp.float32)
    context = (
        context
        + own_prob.astype(jnp.float32)[..., None] * new_values.astype(jnp.float32)[:, :, None, :]
    )
    return context.astype(jnp.bfloat16).reshape(row_count, head_count * head_size)


def near(a):
    return pltpu.with_memory_space_constraint(a, pltpu.VMEM)


def distant(a):
    return pltpu.with_memory_space_constraint(a, pltpu.HBM)


def params():
    return pltpu.CompilerParams(vmem_limit_bytes=LIMIT)


def dot(a, b):
    return jnp.dot(a, b, preferred_element_type=jnp.float32)


def project_kernel(core, context, weight, far, own, buffer, sems):
    def copy(i):
        parity = 1 - core[0] if i < 4 else core[0]
        start = pl.multiple_of((2 * (i % 4) + parity) * BLK, BLK)
        return pltpu.make_async_copy(weight.at[:, pl.ds(start, BLK)], buffer.at[i], sems.at[i])

    for i in range(8):
        copy(i).start()
    for i in range(8):
        copy(i).wait()
        out = far if i < 4 else own
        out[i % 4] = dot(context[...], buffer[i]).astype(out.dtype)


def project(core, context, out_weight):
    rows = context.shape[0]
    return pl.pallas_call(
        project_kernel,
        out_shape=(
            pltpu.VMEM((4, rows, BLK), jnp.bfloat16),
            pltpu.VMEM((4, rows, BLK), jnp.float32),
        ),
        in_specs=[SMEM, VMEM, ANY],
        out_specs=(VMEM, VMEM),
        scratch_shapes=[pltpu.VMEM((8, BLK, BLK), jnp.bfloat16), pltpu.SemaphoreType.DMA((8,))],
        compiler_params=params(),
        cost_estimate=pl.CostEstimate(
            flops=2 * rows * BLK * BLK * 8, bytes_accessed=BLK * BLK * 16, transcendentals=0
        ),
    )(core, near(context), distant(out_weight))


def prepare_kernel(own, one, three, two, tokens, gain, selection, *rest):
    hidden, *outgoing = rest[-5:]
    total = own[...] + tokens[...].astype(jnp.float32)
    for part in (two, one, three):
        total = total + part[...].astype(jnp.float32)
    hidden[...] = total
    scaled = (total * gain[...]).astype(jnp.bfloat16)
    for i, out in enumerate(outgoing):
        out[...] = dot(selection[i], scaled).astype(jnp.bfloat16)


def prepare(own, one, three, two, tokens, gain, selection, swapped):
    rows = tokens.shape[0]
    return pl.pallas_call(
        prepare_kernel,
        out_shape=(pltpu.VMEM((rows, BLK), jnp.float32),)
        + (pltpu.VMEM((CAP, BLK), jnp.bfloat16),) * 4,
        in_specs=[VMEM] * 7 + [ANY] * len(swapped),
        out_specs=(VMEM,) * 5,
        compiler_params=params(),
        cost_estimate=pl.CostEstimate(
            flops=2 * rows * BLK * 4 * CAP, bytes_accessed=1000000, transcendentals=0
        ),
    )(own, one, three, two, tokens, gain, selection, *map(distant, swapped))


def line_rows(index):
    return pl.ds(pl.multiple_of(index * ROWS, ROWS), ROWS)


def squares(piece, inverse):
    value = piece.astype(jnp.float32) * inverse
    value = value * value
    total = value[:, :128]
    for i in range(1, BLK // 128):
        total += value[:, i * 128 : (i + 1) * 128]
    return total


def walk(place, pieces, emit, ready):
    x, y, c = place[0], place[1], place[2]

    def piece(j, i):
        return pieces[j, i * ROWS : (i + 1) * ROWS, :]

    def behind(position, shift):
        return (position - shift + 4) % 4

    @pl.when(c == 0)
    def _():
        blocks = [behind(x, shift) for shift in OFFS]
        for j, shift in enumerate(OFFS):
            ready(j)
            emit(line_rows(behind(y, shift)), [(piece(j, i), k, 2 * k) for i, k in enumerate(blocks)])

    @pl.when(c == 1)
    def _():
        blocks = [behind(x, shift) for shift in OFFS]
        for i, shift in enumerate(OFFS):
            if i == 0:
                for j in range(4):
                    ready(j)
            emit(line_rows(behind(y, shift)), [(piece(j, i), k, 2 * k + 1) for j, k in enumerate(blocks)])


def total_of(terms):
    return functools.reduce(lambda a, b: a + b, terms)


def load(place, given, gate, up, pieces, gate_here, up_here, sems):
    def weight(n):
        source, target = (gate, gate_here) if n < 4 else (up, up_here)
        start = pl.multiple_of((2 * (n % 4) + place[2]) * BLK, BLK)
        return pltpu.make_async_copy(source.at[pl.ds(start, BLK), :], target.at[n % 4], sems.at[n])

    def piece(j):
        return pltpu.make_async_copy(given[j], pieces.at[j], sems.at[8 + j])

    for n in range(8):
        weight(n).start()
    for j in range(4):
        piece(j).start()
    for n in range(8):
        weight(n).wait()
    return lambda j: piece(j).wait()


def enter_far_kernel(place, p0, p1, p2, p3, gate, up, inverse, stats, far, square, *scratch):
    ready = load(place, (p0, p1, p2, p3), gate, up, *scratch)
    pieces, gate_here, up_here, _ = scratch

    def emit(rows, parts):
        far[rows, :HID] = total_of([dot(p, gate_here[k]) for p, k, _ in parts]).astype(far.dtype)
        far[rows, HID : 2 * HID] = total_of([dot(p, up_here[k]) for p, k, _ in parts]).astype(far.dtype)
        sums = total_of([squares(p, inverse[pl.ds(b, 1), :]) for p, _, b in parts])
        far[rows, 2 * HID :] = sums.astype(far.dtype)
        square[rows, :] = sums

    walk(place, pieces, emit, ready)


def enter_own_kernel(place, p0, p1, p2, p3, gate, up, own, *scratch):
    ready = load(place, (p0, p1, p2, p3), gate, up, *scratch)
    pieces, gate_here, up_here, _ = scratch

    def emit(rows, parts):
        own[rows, :HID] = total_of([dot(p, gate_here[k]) for p, k, _ in parts])
        own[rows, HID:] = total_of([dot(p, up_here[k]) for p, k, _ in parts])

    walk(place, pieces, emit, ready)


def enter_scratch():
    return [
        pltpu.VMEM((4, 4 * ROWS, BLK), jnp.bfloat16),
        pltpu.VMEM((4, BLK, HID), jnp.bfloat16),
        pltpu.VMEM((4, BLK, HID), jnp.bfloat16),
        pltpu.SemaphoreType.DMA((12,)),
    ]


def enter_cost():
    return pl.CostEstimate(
        flops=2 * 4 * ROWS * 4 * BLK * 2 * HID, bytes_accessed=7000000, transcendentals=0
    )


def enter_far(place, pieces, gate, up, inverse, stats):
    return pl.pallas_call(
        enter_far_kernel,
        out_shape=(
            pltpu.VMEM((4 * ROWS, 2 * HID + 128), jnp.bfloat16),
            pltpu.VMEM((4 * ROWS, 128), jnp.float32),
        ),
        in_specs=[SMEM] + [ANY] * 6 + [VMEM, ANY],
        out_specs=(VMEM,) * 2,
        scratch_shapes=enter_scratch(),
        compiler_params=params(),
        cost_estimate=enter_cost(),
    )(place, *map(distant, (*pieces, gate, up)), near(inverse), stats)


def enter_own(place, pieces, gate, up):
    return pl.pallas_call(
        enter_own_kernel,
        out_shape=pltpu.VMEM((4 * ROWS, 2 * HID), jnp.float32),
        in_specs=[SMEM] + [ANY] * 6,
        out_specs=VMEM,
        scratch_shapes=enter_scratch(),
        compiler_params=params(),
        cost_estimate=enter_cost(),
    )(place, *map(distant, (*pieces, gate, up)))


def activate_kernel(own, square, far, out):
    for r in range(4):
        rows = slice(r * ROWS, (r + 1) * ROWS)
        other = far[rows, :].astype(jnp.float32)
        mean = jnp.sum(square[rows, :] + other[:, 2 * HID :], axis=1, keepdims=True) * (1.0 / D)
        scale = lax.rsqrt(mean + EPS)
        gate = (own[rows, :HID] + other[:, :HID]) * scale
        upper = (own[rows, HID:] + other[:, HID : 2 * HID]) * scale
        out[rows, :] = (gate * (1.0 / (1.0 + jnp.exp(-gate))) * upper).astype(jnp.bfloat16)


def activate(own, square, far):
    return pl.pallas_call(
        activate_kernel,
        out_shape=pltpu.VMEM((4 * ROWS, HID), jnp.bfloat16),
        in_specs=[VMEM] * 3,
        out_specs=VMEM,
        compiler_params=params(),
    )(near(own), near(square), near(far))


def leave_kernel(wanted, place, act, act_far, down, down_far, *rest):
    outs, (own_here, far_here, sems) = rest[:-3], rest[-3:]
    x, y, c = place[0], place[1], place[2]

    def ahead(position, shift):
        return (position + shift + 4) % 4

    def copies(k):
        start = pl.multiple_of((2 * k + c) * BLK, BLK)
        return (
            pltpu.make_async_copy(down.at[:, pl.ds(start, BLK)], own_here.at[k], sems.at[2 * k]),
            pltpu.make_async_copy(down_far.at[:, pl.ds(start, BLK)], far_here.at[k], sems.at[2 * k + 1]),
        )

    for k in range(4):
        for copy in copies(k):
            copy.start()
    for k in range(4):
        for copy in copies(k):
            copy.wait()

    def term(rows, k):
        return (dot(act[rows, :], own_here[k]) + dot(act_far[rows, :], far_here[k])).astype(jnp.bfloat16)

    for core in range(2):

        @pl.when(c == core)
        def _(core=core):
            for out, (second, firsts) in zip(outs, wanted):
                for i, first in enumerate(firsts):
                    on_x, on_y = (first, second) if core == 0 else (second, first)
                    out[i * ROWS : (i + 1) * ROWS, :] = term(line_rows(ahead(y, on_y)), ahead(x, on_x))


def leave(wanted, place, act, act_far, down, down_far):
    count = sum(len(firsts) for _, firsts in wanted)
    return pl.pallas_call(
        functools.partial(leave_kernel, wanted),
        out_shape=tuple(
            pltpu.VMEM((len(firsts) * ROWS, BLK), jnp.bfloat16) for _, firsts in wanted
        ),
        in_specs=[SMEM, VMEM, VMEM, ANY, ANY],
        out_specs=(VMEM,) * len(wanted),
        scratch_shapes=[
            pltpu.VMEM((4, HID, BLK), jnp.bfloat16),
            pltpu.VMEM((4, HID, BLK), jnp.bfloat16),
            pltpu.SemaphoreType.DMA((8,)),
        ],
        compiler_params=params(),
        cost_estimate=pl.CostEstimate(
            flops=2 * ROWS * count * BLK * 2 * HID, bytes_accessed=4000000, transcendentals=0
        ),
    )(place, near(act), near(act_far), distant(down), distant(down_far))


def slots(routes, expert_count):
    row_count = routes.shape[0]
    expert_ids = jnp.arange(expert_count, dtype=jnp.int32)
    picked = routes[:, :, None] == expert_ids[None, None, :]
    flat = picked.reshape(row_count * 2, expert_count).astype(jnp.int32)
    ranks = (jnp.cumsum(flat, axis=0) - flat).reshape(row_count, 2, expert_count)
    slot_index = jnp.sum(jnp.where(picked, ranks, 0), axis=-1)
    slot_hit = slot_index[:, :, None] == jnp.arange(CAP, dtype=jnp.int32)[None, None, :]
    return picked, picked[:, :, :, None] & slot_hit[:, :, None, :]


def shards(
    tokens,
    queries,
    new_keys,
    new_values,
    key_cache,
    value_cache,
    lengths,
    routes,
    out_weight,
    norm_gain,
    router,
    gate_weight,
    up_weight,
    down_weight,
):
    expert_count = router.shape[1]
    x, y, c = lax.axis_index("x"), lax.axis_index("y"), lax.axis_index("c")
    z = lax.axis_index("z")
    place = jnp.stack([x, y, c]).astype(jnp.int32)
    here = 2 * x + c

    gate_far, up_far, down_far = swap_cores(gate_weight), swap_cores(up_weight), swap_cores(down_weight)
    gain = norm_gain.astype(jnp.float32).reshape(8, BLK)
    inverse = 1.0 / gain

    context = attend_local(queries, new_keys, new_values, key_cache, value_cache, lengths)
    core = c.astype(jnp.int32)[None]
    for_other, for_own = project(core, context, out_weight)
    terms = for_own + swap_cores(for_other).astype(jnp.float32)

    def column(shift):
        return lax.dynamic_index_in_dim(terms, (x + shift + 4) % 4, 0, keepdims=False)

    moved = [along_x(column(shift).astype(jnp.bfloat16), shift) for shift in OFFS[1:]]

    picked, matched = slots(routes, expert_count)
    selection = jnp.any(matched, axis=1).astype(jnp.bfloat16)
    own_gain = lax.dynamic_index_in_dim(gain, here, 0)
    planes = [(z + shift + 4) % 4 for shift in OFFS]
    chosen_rows = jnp.stack(
        [lax.dynamic_index_in_dim(selection, plane, 1, keepdims=False).T for plane in planes]
    )
    hidden, *outgoing = prepare(
        column(0), *moved, tokens, own_gain, chosen_rows, (gate_far, up_far)
    )
    line = jnp.concatenate(
        [outgoing[0]] + [along_z(rows, shift) for rows, shift in zip(outgoing[1:], OFFS[1:])]
    )
    line = jnp.concatenate([line] + [along_first(line, shift) for shift in OFFS[1:]])
    pieces = [line] + [along_second(line, shift) for shift in OFFS[1:]]

    own_router = lax.dynamic_slice_in_dim(router, here * BLK, BLK, 0)
    partial = jnp.concatenate(
        [
            jnp.dot(hidden * own_gain, own_router, precision=lax.Precision.HIGHEST),
            jnp.sum(hidden * hidden, axis=1, keepdims=True),
        ],
        axis=1,
    )
    partial = jnp.pad(partial, ((0, 0), (0, 128 - partial.shape[1])))

    partial = partial + swap_cores(partial)
    stats = partial + along_x(partial, 1) + along_x(partial, -1) + along_x(partial, 2)

    far, square = enter_far(place, pieces, gate_far, up_far, inverse, stats)
    own = enter_own(place, pieces, gate_weight, up_weight)
    act = activate(own, square, swap_cores(far))
    operands = (place, act, swap_cores(act), down_weight, down_far)
    rest = OFFS[1:]
    far2, far1, far3 = leave(((2, rest), (1, rest), (-1, rest)), *operands)
    near2, near1, near3, far0, near0 = leave(
        ((2, (0,)), (1, (0,)), (-1, (0,)), (0, rest), (0, (0,))), *operands
    )

    inverse_rms = lax.rsqrt(stats[:, expert_count : expert_count + 1] * (1.0 / D) + EPS)
    logits = stats[:, :expert_count] * inverse_rms
    chosen = jnp.sum(jnp.where(picked, logits[:, None, :], 0.0), axis=-1)
    first_weight = jax.nn.sigmoid(chosen[:, 0] - chosen[:, 1])
    route_weights = jnp.stack([first_weight, 1.0 - first_weight], axis=1)
    weighted = jnp.sum(jnp.where(matched, route_weights[:, :, None, None], 0.0), axis=1)

    def gathered(own, one, three, two):
        total = own.astype(jnp.float32) + along_second(two, 2).astype(jnp.float32)
        total = total + along_second(one, 1).astype(jnp.float32)
        return total + along_second(three, -1).astype(jnp.float32)

    others = gathered(far0, far1, far3, far2).astype(jnp.bfloat16).reshape(3, ROWS, BLK)
    total = gathered(near0, near1, near3, near2)
    for i, shift in enumerate(rest):
        total = total + along_first(others[i], shift).astype(jnp.float32)
    total = total.reshape(4, CAP, BLK)
    back = total.astype(jnp.bfloat16)
    returned = [total[0]] + [
        along_z(back[i], -shift).astype(jnp.float32) for i, shift in enumerate(OFFS) if i > 0
    ]
    arrived = jnp.stack(returned)
    weighted = jnp.stack(
        [
            lax.dynamic_index_in_dim(weighted, plane, 1, keepdims=False) for plane in planes
        ],
        axis=1,
    )
    mixture = jnp.einsum("rec,ecd->rd", weighted, arrived, precision=lax.Precision.HIGHEST)
    return (hidden + mixture).astype(jnp.bfloat16)


def solution(mesh):
    grid = Mesh(mesh.devices.reshape(4, 4, 4, 2), AXES)
    batch, tp = ("z", "y"), ("x", "c")
    return jax.shard_map(
        shards,
        mesh=grid,
        in_specs=(
            P(batch, tp),
            P(batch, tp, None),
            P(batch, tp, None),
            P(batch, tp, None),
            P(batch, tp, None, None),
            P(batch, tp, None, None),
            P(batch),
            P(batch, None),
            P(tp, None),
            P(),
            P(),
            P(None, (*batch, *tp)),
            P(None, (*batch, *tp)),
            P((*batch, *tp), None),
        ),
        out_specs=P(batch, tp),
        check_vma=False,
    )
```

```python
import functools
import math

import jax
import jax.numpy as jnp
from jax import lax
from jax.experimental import pallas as pl
from jax.experimental.pallas import tpu as pltpu
from jax.sharding import Mesh
from jax.sharding import PartitionSpec as P

CAP = 40
EPS = 1e-05
D = 6144
BLK = 768
ROWS = 160
HID = 256
OFFS = (0, 1, -1, 2)
AXES = ("z", "y", "x", "c")
VMEM = pl.BlockSpec(memory_space=pltpu.VMEM)
ANY = pl.BlockSpec(memory_space=pl.ANY)


def device_index(z, y, x, c):
    return ((z * 4 + y) * 4 + x) * 2 + c


def plane_pairs(first, shift):
    pairs = []
    for z in range(4):
        for y in range(4):
            for x in range(4):
                for c in range(2):
                    if (c == 0) == first:
                        target = device_index(z, y, (x + shift) % 4, c)
                    else:
                        target = device_index(z, (y + shift) % 4, x, c)
                    pairs.append((device_index(z, y, x, c), target))
    return pairs


def along_first(a, shift):
    return lax.ppermute(a, AXES, plane_pairs(True, shift))


def along_second(a, shift):
    return lax.ppermute(a, AXES, plane_pairs(False, shift))


def along_z(a, shift):
    return lax.ppermute(a, "z", [(i, (i + shift) % 4) for i in range(4)])


def along_x(a, shift):
    return lax.ppermute(a, "x", [(i, (i + shift) % 4) for i in range(4)])


def swap_cores(a):
    return lax.ppermute(a, "c", [(0, 1), (1, 0)])


def position():
    return [lax.axis_index(name) for name in ("x", "y", "c", "z")]


def near(a):
    return pltpu.with_memory_space_constraint(a, pltpu.VMEM)


def distant(a):
    return pltpu.with_memory_space_constraint(a, pltpu.HBM)


def params(mebibytes):
    return pltpu.CompilerParams(vmem_limit_bytes=mebibytes * 1024 * 1024)


def dot(a, b):
    return jnp.dot(a, b, preferred_element_type=jnp.float32)


def attend_kernel(
    given_lengths, given_queries, given_keys, given_values, keys, values, weight, far, own,
    lengths, queries, new_keys, new_values, key_here, value_here, weight_here, query_here, score, context, joined,
    sems,
):
    small = [
        pltpu.make_async_copy(source, target, sems.at[16 + n])
        for n, (source, target) in enumerate(
            (
                (given_queries, queries),
                (given_keys, new_keys),
                (given_values, new_values),
                (given_lengths, lengths),
            )
        )
    ]
    for one in small:
        one.start()
    rows, heads, size = queries.shape[1], queries.shape[0], queries.shape[2]
    chunk, core = rows // 4, position()[2]

    def copy(n):
        if n < 8:
            source, target = (keys, key_here) if n < 4 else (values, value_here)
            part = pl.ds(n % 4 * chunk, chunk)
            return pltpu.make_async_copy(source.at[part], target.at[part], sems.at[n])
        parity = 1 - core if n < 12 else core
        start = pl.multiple_of((2 * (n % 4) + parity) * BLK, BLK)
        return pltpu.make_async_copy(weight.at[:, pl.ds(start, BLK)], weight_here.at[n - 8], sems.at[n])

    started = [0]

    def start(count):
        for n in range(started[0], min(count, 16)):
            copy(n).start()
        started[0] = max(started[0], min(count, 16))

    start(6)
    for one in small:
        one.wait()
    query_here[heads * rows :, :] = jnp.zeros(((8 - heads) * rows, size), jnp.float32)
    for head in range(heads):
        query_here[head * rows : (head + 1) * rows, :] = queries[head].astype(jnp.float32)

    def row(t):
        return slice(8 * t, 8 * t + 8)

    scale = 1.0 / math.sqrt(size)
    for n in range(4):
        copy(n).wait()
        start(n + 7)
        for t in range(n * chunk, (n + 1) * chunk):
            query = query_here[pl.ds(t, 8, stride=rows), :]
            score[row(t), :] = scale * lax.dot_general(
                query.astype(jnp.bfloat16), key_here[t],
                (((1,), (1,)), ((), ())), preferred_element_type=jnp.float32,
            )
    slot = lax.broadcasted_iota(jnp.int32, (8, score.shape[1]), 1)
    for n in range(4):
        copy(n + 4).wait()
        start(n + 11)
        for t in range(n * chunk, (n + 1) * chunk):
            query = query_here[pl.ds(t, 8, stride=rows), :]
            new_key = new_keys[t : t + 1, :].astype(jnp.float32)
            mine = scale * jnp.sum(query * new_key, axis=1, keepdims=True)
            scores = score[row(t), :]
            valid = slot < lengths[t]
            top = jnp.maximum(jnp.max(jnp.where(valid, scores, -jnp.inf), axis=1, keepdims=True), mine)
            weights = jnp.where(valid, jnp.exp(scores - top), 0.0)
            own_weight = jnp.exp(mine - top)
            total = jnp.sum(weights, axis=1, keepdims=True) + own_weight
            probs = (weights / total).astype(jnp.bfloat16)
            own_prob = (own_weight / total).astype(jnp.bfloat16).astype(jnp.float32)
            new_value = new_values[t : t + 1, :].astype(jnp.float32)
            context[row(t), :] = dot(probs, value_here[t]) + own_prob * new_value
    for head in range(heads):
        joined[:, head * size : (head + 1) * size] = context[pl.ds(head, rows, stride=8), :].astype(
            jnp.bfloat16
        )
    start(16)
    for n in range(8):
        copy(8 + n).wait()
        out = far if n < 4 else own
        out[n % 4] = dot(joined[...], weight_here[n]).astype(out.dtype)


def attend(lengths, queries, new_keys, new_values, keys, values, out_weight):
    rows, heads, size = queries.shape
    length = keys.shape[2]
    return pl.pallas_call(
        attend_kernel,
        out_shape=(
            pltpu.VMEM((4, rows, BLK), jnp.bfloat16),
            pltpu.VMEM((4, rows, BLK), jnp.float32),
        ),
        in_specs=[ANY] * 7,
        out_specs=(VMEM, VMEM),
        scratch_shapes=[
            pltpu.SMEM((rows,), jnp.int32),
            pltpu.VMEM((heads, rows, size), jnp.bfloat16),
            pltpu.VMEM((rows, size), jnp.bfloat16),
            pltpu.VMEM((rows, size), jnp.bfloat16),
            pltpu.VMEM((rows, length, size), jnp.bfloat16),
            pltpu.VMEM((rows, length, size), jnp.bfloat16),
            pltpu.VMEM((8, BLK, BLK), jnp.bfloat16),
            pltpu.VMEM((8 * rows, size), jnp.float32),
            pltpu.VMEM((8 * rows, length), jnp.float32),
            pltpu.VMEM((8 * rows, size), jnp.float32),
            pltpu.VMEM((rows, heads * size), jnp.bfloat16),
            pltpu.SemaphoreType.DMA((20,)),
        ],
        compiler_params=params(20),
        cost_estimate=pl.CostEstimate(
            flops=2 * rows * BLK * BLK * 8, bytes_accessed=14000000, transcendentals=0
        ),
    )(
        distant(lengths),
        distant(queries.transpose(1, 0, 2)),
        distant(new_keys.reshape(rows, size)),
        distant(new_values.reshape(rows, size)),
        distant(keys.reshape(rows, length, size)),
        distant(values.reshape(rows, length, size)),
        distant(out_weight),
    )


def combine_kernel(own, far, routes, mine, one, three, two, handed):
    handed[...] = routes[...]
    for out, shift in ((mine, 0), (one, 1), (three, -1), (two, 2)):
        block = behind(position()[0], -shift)
        out[...] = (own[block] + far[block].astype(jnp.float32)).astype(out.dtype)


def combine(own, far, routes):
    rows = own.shape[1]
    return pl.pallas_call(
        combine_kernel,
        out_shape=(pltpu.VMEM((rows, BLK), jnp.float32),)
        + (pltpu.VMEM((rows, BLK), jnp.bfloat16),) * 3
        + (jax.ShapeDtypeStruct(routes.shape, routes.dtype),),
        in_specs=[VMEM] * 3,
        out_specs=(VMEM,) * 5,
        compiler_params=params(4),
    )(near(own), near(far), routes)


def slots_kernel(routes, first, second):
    rows = routes.shape[0]
    lane = lax.broadcasted_iota(jnp.int32, (rows, 128), 1)
    plane = jnp.full((rows, 128), -1, jnp.int32)
    for i, shift in enumerate(OFFS):
        plane = jnp.where(lane == i, behind(position()[3], -shift), plane)
    one = jnp.where(routes[:, 0:1] == plane, 1.0, 0.0)
    two = jnp.where(routes[:, 1:2] == plane, 1.0, 0.0)
    before = lax.broadcasted_iota(jnp.int32, (rows, rows), 1) < lax.broadcasted_iota(
        jnp.int32, (rows, rows), 0
    )
    rank = dot(jnp.where(before, 1.0, 0.0).astype(jnp.bfloat16), (one + two).astype(jnp.bfloat16))
    slot = lax.broadcasted_iota(jnp.int32, (rows, CAP), 1).astype(jnp.float32)
    for i in range(4):
        hit = slot == rank[:, i : i + 1]
        first[i] = jnp.where(hit, one[:, i : i + 1], 0.0).astype(jnp.bfloat16)
        second[i] = jnp.where(hit, two[:, i : i + 1], 0.0).astype(jnp.bfloat16)


def slots(routes):
    shape = pltpu.VMEM((4, routes.shape[0], CAP), jnp.bfloat16)
    return pl.pallas_call(
        slots_kernel,
        out_shape=(shape, shape),
        in_specs=[VMEM],
        out_specs=(VMEM, VMEM),
        compiler_params=params(4),
    )(routes)


def prepare_kernel(own, one, three, two, tokens, gain, first, second, *rest):
    hidden, *outgoing = rest[-5:]
    total = own[...] + tokens[...].astype(jnp.float32)
    for part in (two, one, three):
        total = total + part[...].astype(jnp.float32)
    hidden[...] = total
    x, _, c, _ = position()
    scaled = (total * gain[pl.ds(2 * x + c, 1), :]).astype(jnp.bfloat16)
    for i, out in enumerate(outgoing):
        out[...] = lax.dot_general(
            first[i] + second[i], scaled, (((0,), (0,)), ((), ())), preferred_element_type=jnp.float32
        ).astype(jnp.bfloat16)


def prepare(own, one, three, two, tokens, gain, first, second, swapped):
    rows = tokens.shape[0]
    return pl.pallas_call(
        prepare_kernel,
        out_shape=(pltpu.VMEM((rows, BLK), jnp.float32),)
        + (pltpu.VMEM((CAP, BLK), jnp.bfloat16),) * 4,
        in_specs=[VMEM] * 8 + [ANY] * len(swapped),
        out_specs=(VMEM,) * 5,
        compiler_params=params(4),
        cost_estimate=pl.CostEstimate(
            flops=2 * rows * BLK * 4 * CAP, bytes_accessed=1000000, transcendentals=0
        ),
    )(own, one, three, two, tokens, gain, first, second, *map(distant, swapped))


def line_rows(index):
    return pl.ds(pl.multiple_of(index * ROWS, ROWS), ROWS)


def lanes(value):
    total = value[:, :128]
    for i in range(1, BLK // 128):
        total += value[:, i * 128 : (i + 1) * 128]
    return total


def behind(position, shift):
    return (position - shift + 4) % 4


def walk(pieces, emit):
    x, y, c, _ = position()
    blocks = [2 * behind(x, shift) + c for shift in OFFS]

    for core in range(2):

        @pl.when(c == core)
        def _(core=core):
            for m, shift in enumerate(OFFS):

                def found(n, m=m):
                    j, i = (m, n) if core == 0 else (n, m)
                    return pieces[j, i * ROWS : (i + 1) * ROWS, :]

                emit(line_rows(behind(y, shift)), found, blocks, m, core)


def stage_kernel(gate_far, up_far, gate, up, weights, sems):
    x, _, c, _ = position()
    copies = []
    for which, source in enumerate((gate_far, up_far, gate, up)):
        for n, shift in enumerate(OFFS):
            start = pl.multiple_of((2 * behind(x, shift) + c) * BLK, BLK)
            copies.append(
                pltpu.make_async_copy(
                    source.at[pl.ds(start, BLK), :], weights.at[which, n], sems.at[4 * which + n]
                )
            )
    for copy in copies:
        copy.start()
    for copy in copies:
        copy.wait()


def stage(gate_far, up_far, gate, up):
    return pl.pallas_call(
        stage_kernel,
        out_shape=pltpu.VMEM((4, 4, BLK, HID), jnp.bfloat16),
        in_specs=[ANY] * 4,
        out_specs=VMEM,
        scratch_shapes=[pltpu.SemaphoreType.DMA((16,))],
        compiler_params=params(8),
        cost_estimate=pl.CostEstimate(flops=0, bytes_accessed=12000000, transcendentals=0),
    )(*map(distant, (gate_far, up_far, gate, up)))


def enter_kernel(p0, p1, p2, p3, weights, inverse, route, own, sums, far, pieces, sems):
    given = (p0, p1, p2, p3)

    def line(core, m):
        copies = []
        for n in range(4):
            j, i = (m, n) if core == 0 else (n, m)
            rows = pl.ds(i * ROWS, ROWS)
            copies.append(
                pltpu.make_async_copy(given[j].at[rows, :], pieces.at[j, rows, :], sems.at[4 * j + i])
            )
        return copies

    def start(core, m):
        for copy in line(core, m):
            copy.start()

    def product(found, which):
        total = dot(found(0), weights[which, 0])
        for n in range(1, 4):
            total += dot(found(n), weights[which, n])
        return total

    def emit_far(rows, found, blocks, m, core):
        if m == 0:
            start(core, 0)
            start(core, 1)
        for copy in line(core, m):
            copy.wait()
        if m < 2:
            start(core, m + 2)
        far[rows, :HID] = product(found, 0).astype(far.dtype)
        far[rows, HID : 2 * HID] = product(found, 1).astype(far.dtype)
        for n, index in enumerate(blocks):
            value = found(n).astype(jnp.float32)
            plain = value * inverse[pl.ds(index, 1), :]
            terms = lanes(plain * plain), lanes(value * route[pl.ds(index, 1), :])
            totals = terms if n == 0 else [a + b for a, b in zip(totals, terms)]
        for n, total in enumerate(totals):
            sums[rows, n * 128 : (n + 1) * 128] = total
            far[rows, 2 * HID + n * 128 : 2 * HID + (n + 1) * 128] = total.astype(far.dtype)

    def emit_own(rows, found, blocks, m, core):
        own[rows, :HID] = product(found, 2)
        own[rows, HID:] = product(found, 3)

    walk(pieces, emit_far)
    walk(pieces, emit_own)


def enter(pieces, weights, inverse, route):
    return pl.pallas_call(
        enter_kernel,
        out_shape=(
            pltpu.VMEM((4 * ROWS, 2 * HID), jnp.float32),
            pltpu.VMEM((4 * ROWS, 256), jnp.float32),
            pltpu.VMEM((4 * ROWS, 2 * HID + 256), jnp.bfloat16),
        ),
        in_specs=[ANY] * 4 + [VMEM] * 3,
        out_specs=(VMEM,) * 3,
        scratch_shapes=[
            pltpu.VMEM((4, 4 * ROWS, BLK), jnp.bfloat16),
            pltpu.SemaphoreType.DMA((16,)),
        ],
        compiler_params=params(16),
        cost_estimate=pl.CostEstimate(
            flops=2 * 4 * ROWS * 4 * BLK * 4 * HID, bytes_accessed=10000000, transcendentals=0
        ),
    )(*map(distant, pieces), near(weights), near(inverse), near(route))


def activate_kernel(own, sums, far, out, logit):
    for r in range(4):
        rows = slice(r * ROWS, (r + 1) * ROWS)
        other = far[rows, :].astype(jnp.float32)
        both = sums[rows, :] + other[:, 2 * HID :]
        mean = jnp.sum(both[:, :128], axis=1, keepdims=True) * (1.0 / D)
        scale = lax.rsqrt(mean + EPS)
        gate = (own[rows, :HID] + other[:, :HID]) * scale
        upper = (own[rows, HID:] + other[:, HID : 2 * HID]) * scale
        out[rows, :] = (gate * (1.0 / (1.0 + jnp.exp(-gate))) * upper).astype(jnp.bfloat16)
        value = jnp.sum(both[:, 128:], axis=1, keepdims=True) * scale
        logit[rows, :] = jnp.broadcast_to(value, (ROWS, 128))


def activate(own, sums, far):
    return pl.pallas_call(
        activate_kernel,
        out_shape=(
            pltpu.VMEM((4 * ROWS, HID), jnp.bfloat16),
            pltpu.VMEM((4 * ROWS, 128), jnp.float32),
        ),
        in_specs=[VMEM] * 3,
        out_specs=(VMEM,) * 2,
        compiler_params=params(6),
    )(near(own), near(sums), near(far))


def leave_kernel(wanted, act, act_far, down, down_far, *rest):
    outs, (own_here, far_here, sems) = rest[:-3], rest[-3:]
    x, y, c, _ = position()

    def ahead(position, shift):
        return (position + shift + 4) % 4

    def copies(n):
        start = pl.multiple_of((2 * ahead(x, OFFS[n]) + c) * BLK, BLK)
        return (
            pltpu.make_async_copy(down.at[:, pl.ds(start, BLK)], own_here.at[n], sems.at[2 * n]),
            pltpu.make_async_copy(down_far.at[:, pl.ds(start, BLK)], far_here.at[n], sems.at[2 * n + 1]),
        )

    def term(rows, n):
        return (dot(act[rows, :], own_here[n]) + dot(act_far[rows, :], far_here[n])).astype(jnp.bfloat16)

    for core in range(2):
        steps = [
            (out, i, *((first, second) if core == 0 else (second, first)))
            for out, (second, firsts) in enumerate(wanted)
            for i, first in enumerate(firsts)
        ]
        order = list(dict.fromkeys(OFFS.index(on_x) for _, _, on_x, _ in steps))

        @pl.when(c == core)
        def _(steps=steps, order=order):
            waited = set()
            for n in order[:2]:
                for copy in copies(n):
                    copy.start()
            for out, i, on_x, on_y in steps:
                n = OFFS.index(on_x)
                if n not in waited:
                    for copy in copies(n):
                        copy.wait()
                    waited.add(n)
                    for later in order[len(waited) + 1 : len(waited) + 2]:
                        for copy in copies(later):
                            copy.start()
                outs[out][i * ROWS : (i + 1) * ROWS, :] = term(line_rows(ahead(y, on_y)), n)


def leave(wanted, act, act_far, down, down_far):
    count = sum(len(firsts) for _, firsts in wanted)
    return pl.pallas_call(
        functools.partial(leave_kernel, wanted),
        out_shape=tuple(
            pltpu.VMEM((len(firsts) * ROWS, BLK), jnp.bfloat16) for _, firsts in wanted
        ),
        in_specs=[VMEM, VMEM, ANY, ANY],
        out_specs=(VMEM,) * len(wanted),
        scratch_shapes=[
            pltpu.VMEM((4, HID, BLK), jnp.bfloat16),
            pltpu.VMEM((4, HID, BLK), jnp.bfloat16),
            pltpu.SemaphoreType.DMA((8,)),
        ],
        compiler_params=params(8),
        cost_estimate=pl.CostEstimate(
            flops=2 * ROWS * count * BLK * 2 * HID, bytes_accessed=4000000, transcendentals=0
        ),
    )(near(act), near(act_far), distant(down), distant(down_far))


def gather_kernel(own, logit, *rest):
    parts, outs = rest[:-4], rest[-4:]
    y = position()[1]
    total = own[...].astype(jnp.float32)
    for part in parts:
        total = total + part[...].astype(jnp.float32)
    for i, out in enumerate(outs):
        out[:, :BLK] = total[i * CAP : (i + 1) * CAP].astype(jnp.bfloat16)
        value = logit[pl.ds(pl.multiple_of(y * ROWS + i * CAP, CAP), CAP), :]
        high = value.astype(jnp.bfloat16)
        low = (value - high.astype(jnp.float32)).astype(jnp.bfloat16)
        lane = lax.broadcasted_iota(jnp.int32, (CAP, 128), 1)
        out[:, BLK:] = jnp.where(lane < 64, high.astype(jnp.float32), low.astype(jnp.float32)).astype(jnp.bfloat16)


def gather(own, parts, logit):
    return pl.pallas_call(
        gather_kernel,
        out_shape=(pltpu.VMEM((CAP, BLK + 128), jnp.bfloat16),) * 4,
        in_specs=[VMEM] * (2 + len(parts)),
        out_specs=(VMEM,) * 4,
        compiler_params=params(6),
        cost_estimate=pl.CostEstimate(flops=2000000, bytes_accessed=2000000, transcendentals=0),
    )(own, near(logit), *parts)


def finish_kernel(hidden, first, second, b0, b1, b2, b3, out):
    def pick(hits):
        return functools.reduce(
            lambda a, b: a + b, [dot(hits[i], block[...]) for i, block in enumerate((b0, b1, b2, b3))]
        )

    one, two = pick(first), pick(second)

    def logit(rows):
        return rows[:, BLK : BLK + 1] + rows[:, BLK + 64 : BLK + 65]

    weight = 1.0 / (1.0 + jnp.exp(logit(two) - logit(one)))
    mixture = weight * one[:, :BLK] + (1.0 - weight) * two[:, :BLK]
    out[...] = (hidden[...] + mixture).astype(jnp.bfloat16)


def finish(hidden, first, second, blocks):
    return pl.pallas_call(
        finish_kernel,
        out_shape=jax.ShapeDtypeStruct(hidden.shape, jnp.bfloat16),
        in_specs=[VMEM] * 7,
        out_specs=VMEM,
        compiler_params=params(6),
        cost_estimate=pl.CostEstimate(flops=40000000, bytes_accessed=2000000, transcendentals=0),
    )(near(hidden), near(first), near(second), *blocks)


def shards(
    tokens,
    queries,
    new_keys,
    new_values,
    key_cache,
    value_cache,
    lengths,
    routes,
    out_weight,
    norm_gain,
    router,
    gate_weight,
    up_weight,
    down_weight,
):
    z = lax.axis_index("z")

    gate_far, up_far, down_far = swap_cores(gate_weight), swap_cores(up_weight), swap_cores(down_weight)
    gain = norm_gain.astype(jnp.float32).reshape(8, BLK)
    inverse = 1.0 / gain

    for_other, for_own = attend(
        lengths, queries, new_keys, new_values, key_cache, value_cache, out_weight
    )
    mine, one, three, two, routes = combine(for_own, swap_cores(for_other), routes)
    moved = [along_x(one, 1), along_x(three, -1), along_x(two, 2)]
    first_hits, second_hits = slots(routes)
    hidden, *outgoing = prepare(
        mine, *moved, tokens, gain, first_hits, second_hits, (gate_far, up_far)
    )
    line = jnp.concatenate(
        [outgoing[0]] + [along_z(rows, shift) for rows, shift in zip(outgoing[1:], OFFS[1:])]
    )
    line = jnp.concatenate([line] + [along_first(line, shift) for shift in OFFS[1:]])
    pieces = [line] + [along_second(line, shift) for shift in OFFS[1:]]

    route = lax.dynamic_index_in_dim(router, z, 1, keepdims=False).reshape(8, BLK)
    own, sums, far = enter(
        pieces, stage(gate_far, up_far, gate_weight, up_weight), inverse, route
    )
    act, logit = activate(own, sums, swap_cores(far))
    operands = (act, swap_cores(act), down_weight, down_far)
    rest = OFFS[1:]
    (far2,) = leave(((2, rest),), *operands)
    far1, far3 = leave(((1, rest), (-1, rest)), *operands)
    near2, near1, near3, far0, near0 = leave(
        ((2, (0,)), (1, (0,)), (-1, (0,)), (0, rest), (0, (0,))), *operands
    )

    def gathered(own, one, three, two):
        total = own.astype(jnp.float32) + along_second(two, 2).astype(jnp.float32)
        total = total + along_second(one, 1).astype(jnp.float32)
        return total + along_second(three, -1).astype(jnp.float32)

    others = gathered(far0, far1, far3, far2).astype(jnp.bfloat16).reshape(3, ROWS, BLK)
    parts = [along_second(near2, 2), along_second(near1, 1), along_second(near3, -1)]
    parts += [along_first(others[i], shift) for i, shift in enumerate(rest)]
    back = gather(near0, parts, logit)
    blocks = [back[0]] + [along_z(block, -shift) for block, shift in zip(back[1:], rest)]
    return finish(hidden, first_hits, second_hits, blocks)


def solution(mesh):
    grid = Mesh(mesh.devices.reshape(4, 4, 4, 2), AXES)
    batch, tp = ("z", "y"), ("x", "c")
    return jax.shard_map(
        shards,
        mesh=grid,
        in_specs=(
            P(batch, tp),
            P(batch, tp, None),
            P(batch, tp, None),
            P(batch, tp, None),
            P(batch, tp, None, None),
            P(batch, tp, None, None),
            P(batch),
            P(batch, None),
            P(tp, None),
            P(),
            P(),
            P(None, (*batch, *tp)),
            P(None, (*batch, *tp)),
            P((*batch, *tp), None),
        ),
        out_specs=P(batch, tp),
        check_vma=False,
    )
```

```python
import functools
import math

import jax
import jax.numpy as jnp
from jax import lax
from jax.experimental import pallas as pl
from jax.experimental.pallas import tpu as pltpu
from jax.sharding import Mesh
from jax.sharding import PartitionSpec as P

CAP = 40
EPS = 1e-05
D = 6144
BLK = 768
ROWS = 160
HID = 256
OFFS = (0, 1, -1, 2)
AXES = ("z", "y", "x", "c")
VMEM = pl.BlockSpec(memory_space=pltpu.VMEM)
ANY = pl.BlockSpec(memory_space=pl.ANY)


def device_index(z, y, x, c):
    return ((z * 4 + y) * 4 + x) * 2 + c


def plane_pairs(first, shift):
    pairs = []
    for z in range(4):
        for y in range(4):
            for x in range(4):
                for c in range(2):
                    if (c == 0) == first:
                        target = device_index(z, y, (x + shift) % 4, c)
                    else:
                        target = device_index(z, (y + shift) % 4, x, c)
                    pairs.append((device_index(z, y, x, c), target))
    return pairs


def along_first(a, shift):
    return lax.ppermute(a, AXES, plane_pairs(True, shift))


def along_second(a, shift):
    return lax.ppermute(a, AXES, plane_pairs(False, shift))


def along_z(a, shift):
    return lax.ppermute(a, "z", [(i, (i + shift) % 4) for i in range(4)])


def along_x(a, shift):
    return lax.ppermute(a, "x", [(i, (i + shift) % 4) for i in range(4)])


def swap_cores(a):
    return lax.ppermute(a, "c", [(0, 1), (1, 0)])


def position():
    return [lax.axis_index(name) for name in ("x", "y", "c", "z")]


def near(a):
    return pltpu.with_memory_space_constraint(a, pltpu.VMEM)


def distant(a):
    return pltpu.with_memory_space_constraint(a, pltpu.HBM)


def params(mebibytes):
    return pltpu.CompilerParams(vmem_limit_bytes=mebibytes * 1024 * 1024)


def dot(a, b):
    return jnp.dot(a, b, preferred_element_type=jnp.float32)


def attend_kernel(
    given_lengths, given_queries, given_keys, given_values, keys, values, weight, far, own,
    lengths, queries, new_keys, new_values, key_here, value_here, weight_here, query_here, score, context, joined,
    sems,
):
    small = [
        pltpu.make_async_copy(source, target, sems.at[16 + n])
        for n, (source, target) in enumerate(
            (
                (given_queries, queries),
                (given_keys, new_keys),
                (given_values, new_values),
                (given_lengths, lengths),
            )
        )
    ]
    for one in small:
        one.start()
    rows, heads, size = queries.shape[1], queries.shape[0], queries.shape[2]
    chunk, core = rows // 4, position()[2]

    def copy(n):
        if n < 8:
            source, target = (keys, key_here) if n < 4 else (values, value_here)
            part = pl.ds(n % 4 * chunk, chunk)
            return pltpu.make_async_copy(source.at[part], target.at[part], sems.at[n])
        parity = 1 - core if n < 12 else core
        start = pl.multiple_of((2 * (n % 4) + parity) * BLK, BLK)
        return pltpu.make_async_copy(weight.at[:, pl.ds(start, BLK)], weight_here.at[n - 8], sems.at[n])

    started = [0]

    def start(count):
        for n in range(started[0], min(count, 16)):
            copy(n).start()
        started[0] = max(started[0], min(count, 16))

    start(6)
    for one in small:
        one.wait()
    query_here[heads * rows :, :] = jnp.zeros(((8 - heads) * rows, size), jnp.float32)
    for head in range(heads):
        query_here[head * rows : (head + 1) * rows, :] = queries[head].astype(jnp.float32)

    def row(t):
        return slice(8 * t, 8 * t + 8)

    scale = 1.0 / math.sqrt(size)
    for n in range(4):
        copy(n).wait()
        start((8, 10, 12, 12)[n])
        for t in range(n * chunk, (n + 1) * chunk):
            query = query_here[pl.ds(t, 8, stride=rows), :]
            score[row(t), :] = scale * lax.dot_general(
                query.astype(jnp.bfloat16), key_here[t],
                (((1,), (1,)), ((), ())), preferred_element_type=jnp.float32,
            )
    slot = lax.broadcasted_iota(jnp.int32, (8, score.shape[1]), 1)
    for n in range(4):
        copy(n + 4).wait()
        start(13 + n)
        for t in range(n * chunk, (n + 1) * chunk):
            query = query_here[pl.ds(t, 8, stride=rows), :]
            new_key = new_keys[t : t + 1, :].astype(jnp.float32)
            mine = scale * jnp.sum(query * new_key, axis=1, keepdims=True)
            scores = score[row(t), :]
            valid = slot < lengths[t]
            top = jnp.maximum(jnp.max(jnp.where(valid, scores, -jnp.inf), axis=1, keepdims=True), mine)
            weights = jnp.where(valid, jnp.exp(scores - top), 0.0)
            own_weight = jnp.exp(mine - top)
            total = jnp.sum(weights, axis=1, keepdims=True) + own_weight
            probs = (weights / total).astype(jnp.bfloat16)
            own_prob = (own_weight / total).astype(jnp.bfloat16).astype(jnp.float32)
            new_value = new_values[t : t + 1, :].astype(jnp.float32)
            context[row(t), :] = dot(probs, value_here[t]) + own_prob * new_value
    for head in range(heads):
        joined[:, head * size : (head + 1) * size] = context[pl.ds(head, rows, stride=8), :].astype(
            jnp.bfloat16
        )
    start(16)
    for n in range(8):
        copy(8 + n).wait()
        out = far if n < 4 else own
        out[n % 4] = dot(joined[...], weight_here[n]).astype(out.dtype)


def attend(lengths, queries, new_keys, new_values, keys, values, out_weight):
    rows, heads, size = queries.shape
    length = keys.shape[2]
    return pl.pallas_call(
        attend_kernel,
        out_shape=(
            pltpu.VMEM((4, rows, BLK), jnp.bfloat16),
            pltpu.VMEM((4, rows, BLK), jnp.float32),
        ),
        in_specs=[ANY] * 7,
        out_specs=(VMEM, VMEM),
        scratch_shapes=[
            pltpu.SMEM((rows,), jnp.int32),
            pltpu.VMEM((heads, rows, size), jnp.bfloat16),
            pltpu.VMEM((rows, size), jnp.bfloat16),
            pltpu.VMEM((rows, size), jnp.bfloat16),
            pltpu.VMEM((rows, length, size), jnp.bfloat16),
            pltpu.VMEM((rows, length, size), jnp.bfloat16),
            pltpu.VMEM((8, BLK, BLK), jnp.bfloat16),
            pltpu.VMEM((8 * rows, size), jnp.float32),
            pltpu.VMEM((8 * rows, length), jnp.float32),
            pltpu.VMEM((8 * rows, size), jnp.float32),
            pltpu.VMEM((rows, heads * size), jnp.bfloat16),
            pltpu.SemaphoreType.DMA((20,)),
        ],
        compiler_params=params(20),
        cost_estimate=pl.CostEstimate(
            flops=2 * rows * BLK * BLK * 8, bytes_accessed=14000000, transcendentals=0
        ),
    )(
        distant(lengths),
        distant(queries.transpose(1, 0, 2)),
        distant(new_keys.reshape(rows, size)),
        distant(new_values.reshape(rows, size)),
        distant(keys.reshape(rows, length, size)),
        distant(values.reshape(rows, length, size)),
        distant(out_weight),
    )


def combine_kernel(own, far, routes, mine, one, three, two, handed):
    handed[...] = routes[...]
    for out, shift in ((mine, 0), (one, 1), (three, -1), (two, 2)):
        block = behind(position()[0], -shift)
        out[...] = (own[block] + far[block].astype(jnp.float32)).astype(out.dtype)


def combine(own, far, routes):
    rows = own.shape[1]
    return pl.pallas_call(
        combine_kernel,
        out_shape=(pltpu.VMEM((rows, BLK), jnp.float32),)
        + (pltpu.VMEM((rows, BLK), jnp.bfloat16),) * 3
        + (jax.ShapeDtypeStruct(routes.shape, routes.dtype),),
        in_specs=[VMEM] * 3,
        out_specs=(VMEM,) * 5,
        compiler_params=params(4),
    )(near(own), near(far), routes)


def slots_kernel(routes, down, first, second, down_half, sems):
    c = position()[2]
    copies = []
    for k in range(4):
        start = pl.multiple_of((2 * k + 1 - c) * BLK, BLK)
        copies.append(pltpu.make_async_copy(down.at[:, pl.ds(start, BLK)], down_half.at[k], sems.at[k]))
        copies[k].start()
    rows = routes.shape[0]
    lane = lax.broadcasted_iota(jnp.int32, (rows, 128), 1)
    plane = jnp.full((rows, 128), -1, jnp.int32)
    for i, shift in enumerate(OFFS):
        plane = jnp.where(lane == i, behind(position()[3], -shift), plane)
    one = jnp.where(routes[:, 0:1] == plane, 1.0, 0.0)
    two = jnp.where(routes[:, 1:2] == plane, 1.0, 0.0)
    before = lax.broadcasted_iota(jnp.int32, (rows, rows), 1) < lax.broadcasted_iota(
        jnp.int32, (rows, rows), 0
    )
    rank = dot(jnp.where(before, 1.0, 0.0).astype(jnp.bfloat16), (one + two).astype(jnp.bfloat16))
    slot = lax.broadcasted_iota(jnp.int32, (rows, CAP), 1).astype(jnp.float32)
    for i in range(4):
        hit = slot == rank[:, i : i + 1]
        first[i] = jnp.where(hit, one[:, i : i + 1], 0.0).astype(jnp.bfloat16)
        second[i] = jnp.where(hit, two[:, i : i + 1], 0.0).astype(jnp.bfloat16)
    for copy in copies:
        copy.wait()


def slots(routes, down):
    shape = pltpu.VMEM((4, routes.shape[0], CAP), jnp.bfloat16)
    return pl.pallas_call(
        slots_kernel,
        out_shape=(shape, shape, pltpu.VMEM((4, HID, BLK), jnp.bfloat16)),
        in_specs=[VMEM, ANY],
        out_specs=(VMEM,) * 3,
        scratch_shapes=[pltpu.SemaphoreType.DMA((4,))],
        compiler_params=params(4),
    )(routes, distant(down))


def prepare_kernel(own, one, three, two, tokens, gain, first, second, *rest):
    hidden, *outgoing = rest[-5:]
    total = own[...] + tokens[...].astype(jnp.float32)
    for part in (two, one, three):
        total = total + part[...].astype(jnp.float32)
    hidden[...] = total
    x, _, c, _ = position()
    scaled = (total * gain[pl.ds(2 * x + c, 1), :]).astype(jnp.bfloat16)
    for i, out in enumerate(outgoing):
        out[...] = lax.dot_general(
            first[i] + second[i], scaled, (((0,), (0,)), ((), ())), preferred_element_type=jnp.float32
        ).astype(jnp.bfloat16)


def prepare(own, one, three, two, tokens, gain, first, second, swapped):
    rows = tokens.shape[0]
    return pl.pallas_call(
        prepare_kernel,
        out_shape=(pltpu.VMEM((rows, BLK), jnp.float32),)
        + (pltpu.VMEM((CAP, BLK), jnp.bfloat16),) * 4,
        in_specs=[VMEM] * 8 + [ANY] * len(swapped),
        out_specs=(VMEM,) * 5,
        compiler_params=params(4),
        cost_estimate=pl.CostEstimate(
            flops=2 * rows * BLK * 4 * CAP, bytes_accessed=1000000, transcendentals=0
        ),
    )(own, one, three, two, tokens, gain, first, second, *map(distant, swapped))


def join_kernel(a, b, c, d, token, out):
    for i, part in enumerate((a, b, c, d)):
        out[i * ROWS : (i + 1) * ROWS, :] = part[...]


def join(parts):
    token = swap_cores(sum(part[:16, :128].astype(jnp.float32) for part in parts[1:]))
    return pl.pallas_call(
        join_kernel,
        out_shape=pltpu.VMEM((4 * ROWS, BLK), jnp.bfloat16),
        in_specs=[VMEM] * 4 + [ANY],
        out_specs=VMEM,
        compiler_params=params(4),
        cost_estimate=pl.CostEstimate(flops=0, bytes_accessed=2000000, transcendentals=0),
    )(*parts, token)


def line_rows(index):
    return pl.ds(pl.multiple_of(index * ROWS, ROWS), ROWS)


def lanes(value):
    total = value[:, :128]
    for i in range(1, BLK // 128):
        total += value[:, i * 128 : (i + 1) * 128]
    return total


def behind(position, shift):
    return (position - shift + 4) % 4


def walk(held, emit):
    x, y, c, _ = position()
    blocks = [2 * behind(x, shift) + c for shift in OFFS]

    for core in range(2):

        @pl.when(c == core)
        def _(core=core):
            for m, shift in enumerate(OFFS):
                if core == 0:
                    spots = {n: (held.index(m), n) for n in range(4)} if m in held else {}
                else:
                    spots = {n: (j, m) for j, n in enumerate(held)}
                emit(core, line_rows(behind(y, shift)), m, blocks, spots)


def stage_kernel(gate_far, up_far, gate, up, down, down_far, weights, downs, sems):
    x, _, c, _ = position()
    copies = []
    for n, shift in enumerate(OFFS):
        rows = pl.ds(pl.multiple_of((2 * behind(x, shift) + c) * BLK, BLK), BLK)
        columns = pl.ds(pl.multiple_of((2 * behind(x, -shift) + c) * BLK, BLK), BLK)
        for which, source in enumerate((gate_far, up_far, gate, up)):
            copies.append((source.at[rows, :], weights.at[which, n]))
        copies.append((down.at[:, columns], downs.at[0, n]))
        copies.append((down_far.at[behind(x, -shift)], downs.at[1, n]))
    copies = [pltpu.make_async_copy(*ends, sems.at[i]) for i, ends in enumerate(copies)]
    for copy in copies:
        copy.start()
    for copy in copies:
        copy.wait()


def stage(*sources):
    return pl.pallas_call(
        stage_kernel,
        out_shape=(
            pltpu.VMEM((4, 4, BLK, HID), jnp.bfloat16),
            pltpu.VMEM((2, 4, HID, BLK), jnp.bfloat16),
        ),
        in_specs=[ANY] * 6,
        out_specs=(VMEM, VMEM),
        scratch_shapes=[pltpu.SemaphoreType.DMA((24,))],
        compiler_params=params(12),
        cost_estimate=pl.CostEstimate(flops=0, bytes_accessed=18000000, transcendentals=0),
    )(*map(distant, sources))


def enter_terms(pieces, weights, inverse, route, blocks, spots):
    def found(n):
        j, i = spots[n]
        return pieces[j, i * ROWS : (i + 1) * ROWS, :]

    def total(terms):
        return functools.reduce(lambda a, b: a + b, terms)

    sums = [total([dot(found(n), weights[which, n]) for n in spots]) for which in range(4)]
    squares, products = [], []
    for n in spots:
        value = found(n).astype(jnp.float32)
        plain = value * inverse[pl.ds(blocks[n], 1), :]
        squares.append(lanes(plain * plain))
        products.append(lanes(value * route[pl.ds(blocks[n], 1), :]))
    return sums, (total(squares), total(products))


def put(ref, rows, values):
    start = 0
    for value in values:
        ref[rows, start : start + value.shape[1]] = value.astype(ref.dtype)
        start += value.shape[1]


def enter_first_kernel(p0, p1, weights, inverse, route, own, sums, far, pieces, sems):
    copies = [pltpu.make_async_copy(p, pieces.at[j], sems.at[j]) for j, p in enumerate((p0, p1))]
    for copy in copies:
        copy.start()
    for copy in copies:
        copy.wait()

    def emit(core, rows, m, blocks, spots):
        if spots:
            terms, both = enter_terms(pieces, weights, inverse, route, blocks, spots)
            put(far, rows, terms[:2])
            put(own, rows, terms[2:])
            put(sums, rows, both)

    walk((0, 3), emit)


def enter_second_kernel(
    p0, p1, weights, inverse, route, own_first, sums_first, far_first, own, sums, far, pieces, sems
):
    given = (p0, p1)

    def copies(core, step):
        parts = []
        for j in range(2):
            if core == 0 and j == step or core == 1:
                rows = pl.ds(0, 4 * ROWS) if core == 0 else pl.ds(step * ROWS, ROWS)
                parts.append(
                    pltpu.make_async_copy(given[j].at[rows, :], pieces.at[j, rows, :], sems.at[4 * j + step])
                )
        return parts

    def start(core, step):
        for copy in copies(core, step):
            copy.start()

    def wait(core, step):
        for copy in copies(core, step):
            copy.wait()

    def emit(core, rows, m, blocks, spots):
        if m == 0:
            start(core, 0)
            start(core, 1)
        if core == 0 and m in (1, 2):
            wait(core, m - 1)
        if core == 1:
            wait(core, m)
            if m < 2:
                start(core, m + 2)
        before = (far_first[rows, :], own_first[rows, :], sums_first[rows, :])
        if not spots:
            far_all, own_all, both = before
        else:
            terms, both = enter_terms(pieces, weights, inverse, route, blocks, spots)
            far_all, own_all, both = (jnp.concatenate(v, axis=1) for v in (terms[:2], terms[2:], both))
            if core == 1:
                far_all, own_all, both = far_all + before[0], own_all + before[1], both + before[2]
        own[rows, :] = own_all
        sums[rows, :] = both
        put(far, rows, (far_all, both))

    walk((1, 2), emit)


def enter(pieces, weights, inverse, route):
    own = pltpu.VMEM((4 * ROWS, 2 * HID), jnp.float32)
    sums = pltpu.VMEM((4 * ROWS, 256), jnp.float32)
    cost = pl.CostEstimate(
        flops=2 * 4 * ROWS * 2 * BLK * 4 * HID, bytes_accessed=5000000, transcendentals=0
    )
    scratch = [pltpu.VMEM((2, 4 * ROWS, BLK), jnp.bfloat16), pltpu.SemaphoreType.DMA((8,))]
    fixed = (near(weights), near(inverse), near(route))
    first = pl.pallas_call(
        enter_first_kernel,
        out_shape=(own, sums, own),
        in_specs=[ANY] * 2 + [VMEM] * 3,
        out_specs=(VMEM,) * 3,
        scratch_shapes=scratch,
        compiler_params=params(10),
        cost_estimate=cost,
    )(distant(pieces[0]), distant(pieces[3]), *fixed)
    return pl.pallas_call(
        enter_second_kernel,
        out_shape=(own, sums, pltpu.VMEM((4 * ROWS, 2 * HID + 256), jnp.bfloat16)),
        in_specs=[ANY] * 2 + [VMEM] * 6,
        out_specs=(VMEM,) * 3,
        scratch_shapes=scratch,
        compiler_params=params(10),
        cost_estimate=cost,
    )(distant(pieces[1]), distant(pieces[2]), *fixed, *map(near, first))


def activate_kernel(own, sums, far, out, logit):
    for r in range(4):
        rows = slice(r * ROWS, (r + 1) * ROWS)
        other = far[rows, :].astype(jnp.float32)
        both = sums[rows, :] + other[:, 2 * HID :]
        mean = jnp.sum(both[:, :128], axis=1, keepdims=True) * (1.0 / D)
        scale = lax.rsqrt(mean + EPS)
        gate = (own[rows, :HID] + other[:, :HID]) * scale
        upper = (own[rows, HID:] + other[:, HID : 2 * HID]) * scale
        out[rows, :] = (gate * (1.0 / (1.0 + jnp.exp(-gate))) * upper).astype(jnp.bfloat16)
        value = jnp.sum(both[:, 128:], axis=1, keepdims=True) * scale
        logit[rows, :] = jnp.broadcast_to(value, (ROWS, 128))


def activate(own, sums, far):
    return pl.pallas_call(
        activate_kernel,
        out_shape=(
            pltpu.VMEM((4 * ROWS, HID), jnp.bfloat16),
            pltpu.VMEM((4 * ROWS, 128), jnp.float32),
        ),
        in_specs=[VMEM] * 3,
        out_specs=(VMEM,) * 2,
        compiler_params=params(6),
    )(near(own), near(sums), near(far))


def leave_kernel(wanted, act, act_far, downs, *outs):
    _, y, c, _ = position()

    for core in range(2):

        @pl.when(c == core)
        def _(core=core):
            for out, (second, firsts) in zip(outs, wanted):
                for i, first in enumerate(firsts):
                    on_x, on_y = (first, second) if core == 0 else (second, first)
                    rows, n = line_rows(behind(y, -on_y)), OFFS.index(on_x)
                    value = dot(act[rows, :], downs[0, n]) + dot(act_far[rows, :], downs[1, n])
                    out[i * ROWS : (i + 1) * ROWS, :] = value.astype(jnp.bfloat16)


def leave(wanted, act, act_far, downs):
    count = sum(len(firsts) for _, firsts in wanted)
    return pl.pallas_call(
        functools.partial(leave_kernel, wanted),
        out_shape=tuple(
            pltpu.VMEM((len(firsts) * ROWS, BLK), jnp.bfloat16) for _, firsts in wanted
        ),
        in_specs=[VMEM] * 3,
        out_specs=(VMEM,) * len(wanted),
        compiler_params=params(6),
        cost_estimate=pl.CostEstimate(
            flops=2 * ROWS * count * BLK * 2 * HID, bytes_accessed=4000000, transcendentals=0
        ),
    )(near(act), near(act_far), near(downs))


def gather_kernel(own, logit, *rest):
    parts, outs = rest[:-4], rest[-4:]
    y = position()[1]
    total = own[...].astype(jnp.float32)
    for part in parts:
        total = total + part[...].astype(jnp.float32)
    for i, out in enumerate(outs):
        out[:, :BLK] = total[i * CAP : (i + 1) * CAP].astype(jnp.bfloat16)
        value = logit[pl.ds(pl.multiple_of(y * ROWS + i * CAP, CAP), CAP), :]
        high = value.astype(jnp.bfloat16)
        low = (value - high.astype(jnp.float32)).astype(jnp.bfloat16)
        lane = lax.broadcasted_iota(jnp.int32, (CAP, 128), 1)
        out[:, BLK:] = jnp.where(lane < 64, high.astype(jnp.float32), low.astype(jnp.float32)).astype(jnp.bfloat16)


def gather(own, parts, logit):
    return pl.pallas_call(
        gather_kernel,
        out_shape=(pltpu.VMEM((CAP, BLK + 128), jnp.bfloat16),) * 4,
        in_specs=[VMEM] * (2 + len(parts)),
        out_specs=(VMEM,) * 4,
        compiler_params=params(6),
        cost_estimate=pl.CostEstimate(flops=2000000, bytes_accessed=2000000, transcendentals=0),
    )(own, near(logit), *parts)


def finish_kernel(hidden, first, second, b0, b1, b2, b3, out):
    def pick(hits):
        return functools.reduce(
            lambda a, b: a + b, [dot(hits[i], block[...]) for i, block in enumerate((b0, b1, b2, b3))]
        )

    one, two = pick(first), pick(second)

    def logit(rows):
        return rows[:, BLK : BLK + 1] + rows[:, BLK + 64 : BLK + 65]

    weight = 1.0 / (1.0 + jnp.exp(logit(two) - logit(one)))
    mixture = weight * one[:, :BLK] + (1.0 - weight) * two[:, :BLK]
    out[...] = (hidden[...] + mixture).astype(jnp.bfloat16)


def finish(hidden, first, second, blocks):
    return pl.pallas_call(
        finish_kernel,
        out_shape=jax.ShapeDtypeStruct(hidden.shape, jnp.bfloat16),
        in_specs=[VMEM] * 7,
        out_specs=VMEM,
        compiler_params=params(6),
        cost_estimate=pl.CostEstimate(flops=40000000, bytes_accessed=2000000, transcendentals=0),
    )(near(hidden), near(first), near(second), *blocks)


def shards(
    tokens,
    queries,
    new_keys,
    new_values,
    key_cache,
    value_cache,
    lengths,
    routes,
    out_weight,
    norm_gain,
    router,
    gate_weight,
    up_weight,
    down_weight,
):
    z = lax.axis_index("z")

    gate_far, up_far = swap_cores(gate_weight), swap_cores(up_weight)
    gain = norm_gain.astype(jnp.float32).reshape(8, BLK)
    inverse = 1.0 / gain

    for_other, for_own = attend(
        lengths, queries, new_keys, new_values, key_cache, value_cache, out_weight
    )
    mine, one, three, two, routes = combine(for_own, swap_cores(for_other), routes)
    moved = [along_x(one, 1), along_x(three, -1), along_x(two, 2)]
    first_hits, second_hits, down_half = slots(routes, down_weight)
    down_far = swap_cores(down_half)
    hidden, *outgoing = prepare(
        mine, *moved, tokens, gain, first_hits, second_hits, (gate_far, up_far)
    )
    line = jnp.concatenate(
        [outgoing[0]] + [along_z(rows, shift) for rows, shift in zip(outgoing[1:], OFFS[1:])]
    )
    line = join([line] + [along_first(line, shift) for shift in OFFS[1:]])
    pieces = [line] + [along_second(line, shift) for shift in OFFS[1:]]

    route = lax.dynamic_index_in_dim(router, z, 1, keepdims=False).reshape(8, BLK)
    weights, downs = stage(gate_far, up_far, gate_weight, up_weight, down_weight, down_far)
    own, sums, far = enter(pieces, weights, inverse, route)
    act, logit = activate(own, sums, swap_cores(far))
    operands = (act, swap_cores(act), downs)
    rest = OFFS[1:]
    (far2,) = leave(((2, rest),), *operands)
    far1, far3 = leave(((1, rest), (-1, rest)), *operands)
    near2, near1, near3, far0, near0 = leave(
        ((2, (0,)), (1, (0,)), (-1, (0,)), (0, rest), (0, (0,))), *operands
    )

    def gathered(own, one, three, two):
        total = own.astype(jnp.float32) + along_second(two, 2).astype(jnp.float32)
        total = total + along_second(one, 1).astype(jnp.float32)
        return total + along_second(three, -1).astype(jnp.float32)

    others = gathered(far0, far1, far3, far2).astype(jnp.bfloat16).reshape(3, ROWS, BLK)
    parts = [along_second(near2, 2), along_second(near1, 1), along_second(near3, -1)]
    parts += [along_first(others[i], shift) for i, shift in enumerate(rest)]
    back = gather(near0, parts, logit)
    blocks = [back[0]] + [along_z(block, -shift) for block, shift in zip(back[1:], rest)]
    return finish(hidden, first_hits, second_hits, blocks)


def solution(mesh):
    grid = Mesh(mesh.devices.reshape(4, 4, 4, 2), AXES)
    batch, tp = ("z", "y"), ("x", "c")
    return jax.shard_map(
        shards,
        mesh=grid,
        in_specs=(
            P(batch, tp),
            P(batch, tp, None),
            P(batch, tp, None),
            P(batch, tp, None),
            P(batch, tp, None, None),
            P(batch, tp, None, None),
            P(batch),
            P(batch, None),
            P(tp, None),
            P(),
            P(),
            P(None, (*batch, *tp)),
            P(None, (*batch, *tp)),
            P((*batch, *tp), None),
        ),
        out_specs=P(batch, tp),
        check_vma=False,
    )
```

```python
import functools
import math

import jax
import jax.numpy as jnp
from jax import lax
from jax.experimental import pallas as pl
from jax.experimental.pallas import tpu as pltpu
from jax.sharding import Mesh
from jax.sharding import PartitionSpec as P

CAP = 40
EPS = 1e-05
D = 6144
BLK = 768
ROWS = 160
HID = 256
OFFS = (0, 1, 3, 2)
AXES = ("z", "y", "x", "c")
VMEM = pl.BlockSpec(memory_space=pltpu.VMEM)
ANY = pl.BlockSpec(memory_space=pl.ANY)


def device_index(z, y, x, c):
    return ((z * 4 + y) * 4 + x) * 2 + c


def plane_pairs(first, shift):
    pairs = []
    for z in range(4):
        for y in range(4):
            for x in range(4):
                for c in range(2):
                    if (c == 0) == first:
                        target = device_index(z, y, x ^ shift, c)
                    else:
                        target = device_index(z, y ^ shift, x, c)
                    pairs.append((device_index(z, y, x, c), target))
    return pairs


def along_first(a, shift):
    return lax.ppermute(a, AXES, plane_pairs(True, shift))


def along_second(a, shift):
    return lax.ppermute(a, AXES, plane_pairs(False, shift))


def along_z(a, shift):
    return lax.ppermute(a, "z", [(i, i ^ shift) for i in range(4)])


def along_x(a, shift):
    return lax.ppermute(a, "x", [(i, i ^ shift) for i in range(4)])


def swap_cores(a):
    return lax.ppermute(a, "c", [(0, 1), (1, 0)])


def position():
    return [lax.axis_index(name) for name in ("x", "y", "c", "z")]


def near(a):
    return pltpu.with_memory_space_constraint(a, pltpu.VMEM)


def distant(a):
    return pltpu.with_memory_space_constraint(a, pltpu.HBM)


def params(mebibytes):
    return pltpu.CompilerParams(vmem_limit_bytes=mebibytes * 1024 * 1024)


def dot(a, b):
    return jnp.dot(a, b, preferred_element_type=jnp.float32)


def attend_kernel(
    given_lengths, given_queries, given_keys, given_values, keys, values, weight, far, joined,
    lengths, queries, new_keys, new_values, key_here, value_here, weight_here, query_here, score, context, sems,
):
    small = [
        pltpu.make_async_copy(source, target, sems.at[16 + n])
        for n, (source, target) in enumerate(
            (
                (given_queries, queries),
                (given_keys, new_keys),
                (given_values, new_values),
                (given_lengths, lengths),
            )
        )
    ]
    for one in small:
        one.start()
    rows, heads, size = queries.shape[1], queries.shape[0], queries.shape[2]
    chunk, core = rows // 4, position()[2]

    def copy(n):
        if n < 8:
            source, target = (keys, key_here) if n < 4 else (values, value_here)
            part = pl.ds(n % 4 * chunk, chunk)
            return pltpu.make_async_copy(source.at[part], target.at[part], sems.at[n])
        start = pl.multiple_of((2 * (n % 4) + 1 - core) * BLK, BLK)
        return pltpu.make_async_copy(weight.at[:, pl.ds(start, BLK)], weight_here.at[n - 8], sems.at[n])

    started = [0]

    def start(until):
        for n in range(started[0], until):
            copy(n).start()
        started[0] = max(started[0], until)

    start(6)
    for one in small:
        one.wait()
    query_here[heads * rows :, :] = jnp.zeros(((8 - heads) * rows, size), jnp.float32)
    for head in range(heads):
        query_here[head * rows : (head + 1) * rows, :] = queries[head].astype(jnp.float32)

    def row(t):
        return slice(8 * t, 8 * t + 8)

    scale = 1.0 / math.sqrt(size)
    for n in range(4):
        copy(n).wait()
        start((8, 9, 10, 11)[n])
        for t in range(n * chunk, (n + 1) * chunk):
            query = query_here[pl.ds(t, 8, stride=rows), :]
            score[row(t), :] = scale * lax.dot_general(
                query.astype(jnp.bfloat16), key_here[t],
                (((1,), (1,)), ((), ())), preferred_element_type=jnp.float32,
            )
    slot = lax.broadcasted_iota(jnp.int32, (8, score.shape[1]), 1)
    for n in range(4):
        copy(n + 4).wait()
        start(12)
        for t in range(n * chunk, (n + 1) * chunk):
            query = query_here[pl.ds(t, 8, stride=rows), :]
            new_key = new_keys[t : t + 1, :].astype(jnp.float32)
            mine = scale * jnp.sum(query * new_key, axis=1, keepdims=True)
            scores = score[row(t), :]
            valid = slot < lengths[t]
            top = jnp.maximum(jnp.max(jnp.where(valid, scores, -jnp.inf), axis=1, keepdims=True), mine)
            weights = jnp.where(valid, jnp.exp(scores - top), 0.0)
            own_weight = jnp.exp(mine - top)
            total = jnp.sum(weights, axis=1, keepdims=True) + own_weight
            probs = (weights / total).astype(jnp.bfloat16)
            own_prob = (own_weight / total).astype(jnp.bfloat16).astype(jnp.float32)
            new_value = new_values[t : t + 1, :].astype(jnp.float32)
            context[row(t), :] = dot(probs, value_here[t]) + own_prob * new_value
    for head in range(heads):
        joined[:, head * size : (head + 1) * size] = context[pl.ds(head, rows, stride=8), :].astype(
            jnp.bfloat16
        )
    for n in range(4):
        copy(8 + n).wait()
        far[n] = dot(joined[...], weight_here[n]).astype(far.dtype)


def attend(lengths, queries, new_keys, new_values, keys, values, out_weight):
    rows, heads, size = queries.shape
    length = keys.shape[2]
    return pl.pallas_call(
        attend_kernel,
        out_shape=(
            pltpu.VMEM((4, rows, BLK), jnp.bfloat16),
            pltpu.VMEM((rows, heads * size), jnp.bfloat16),
        ),
        in_specs=[ANY] * 7,
        out_specs=(VMEM, VMEM),
        scratch_shapes=[
            pltpu.SMEM((rows,), jnp.int32),
            pltpu.VMEM((heads, rows, size), jnp.bfloat16),
            pltpu.VMEM((rows, size), jnp.bfloat16),
            pltpu.VMEM((rows, size), jnp.bfloat16),
            pltpu.VMEM((rows, length, size), jnp.bfloat16),
            pltpu.VMEM((rows, length, size), jnp.bfloat16),
            pltpu.VMEM((4, BLK, BLK), jnp.bfloat16),
            pltpu.VMEM((8 * rows, size), jnp.float32),
            pltpu.VMEM((8 * rows, length), jnp.float32),
            pltpu.VMEM((8 * rows, size), jnp.float32),
            pltpu.SemaphoreType.DMA((20,)),
        ],
        compiler_params=params(20),
        cost_estimate=pl.CostEstimate(
            flops=2 * rows * BLK * BLK * 8, bytes_accessed=14000000, transcendentals=0
        ),
    )(
        distant(lengths),
        distant(queries.transpose(1, 0, 2)),
        distant(new_keys.reshape(rows, size)),
        distant(new_values.reshape(rows, size)),
        distant(keys.reshape(rows, length, size)),
        distant(values.reshape(rows, length, size)),
        distant(out_weight),
    )


def project_kernel(context, weight, own, weight_here, sems):
    core = position()[2]
    copies = []
    for n in range(4):
        start = pl.multiple_of((2 * n + core) * BLK, BLK)
        copies.append(
            pltpu.make_async_copy(weight.at[:, pl.ds(start, BLK)], weight_here.at[n], sems.at[n])
        )
    for copy in copies:
        copy.start()
    for n in range(4):
        copies[n].wait()
        own[n] = dot(context[...], weight_here[n])


def project(context, out_weight):
    rows = context.shape[0]
    return pl.pallas_call(
        project_kernel,
        out_shape=pltpu.VMEM((4, rows, BLK), jnp.float32),
        in_specs=[VMEM, ANY],
        out_specs=VMEM,
        scratch_shapes=[pltpu.VMEM((4, BLK, BLK), jnp.bfloat16), pltpu.SemaphoreType.DMA((4,))],
        compiler_params=params(8),
        cost_estimate=pl.CostEstimate(
            flops=2 * rows * BLK * BLK * 4, bytes_accessed=5000000, transcendentals=0
        ),
    )(near(context), distant(out_weight))


def combine_kernel(own, far, routes, mine, one, three, two, handed):
    handed[...] = routes[...]
    for out, shift in ((mine, 0), (one, 1), (three, 3), (two, 2)):
        block = partner(position()[0], shift)
        out[...] = (own[block] + far[block].astype(jnp.float32)).astype(out.dtype)


def combine(own, far, routes):
    rows = own.shape[1]
    return pl.pallas_call(
        combine_kernel,
        out_shape=(pltpu.VMEM((rows, BLK), jnp.float32),)
        + (pltpu.VMEM((rows, BLK), jnp.bfloat16),) * 3
        + (jax.ShapeDtypeStruct(routes.shape, routes.dtype),),
        in_specs=[VMEM] * 3,
        out_specs=(VMEM,) * 5,
        compiler_params=params(4),
    )(near(own), near(far), routes)


def slots_kernel(routes, down, first, second, down_half, sems):
    c = position()[2]
    copies = []
    for k in range(4):
        start = pl.multiple_of((2 * k + 1 - c) * BLK, BLK)
        copies.append(pltpu.make_async_copy(down.at[:, pl.ds(start, BLK)], down_half.at[k], sems.at[k]))
        copies[k].start()
    rows = routes.shape[0]
    lane = lax.broadcasted_iota(jnp.int32, (rows, 128), 1)
    plane = jnp.full((rows, 128), -1, jnp.int32)
    for i, shift in enumerate(OFFS):
        plane = jnp.where(lane == i, partner(position()[3], shift), plane)
    one = jnp.where(routes[:, 0:1] == plane, 1.0, 0.0)
    two = jnp.where(routes[:, 1:2] == plane, 1.0, 0.0)
    before = lax.broadcasted_iota(jnp.int32, (rows, rows), 1) < lax.broadcasted_iota(
        jnp.int32, (rows, rows), 0
    )
    rank = dot(jnp.where(before, 1.0, 0.0).astype(jnp.bfloat16), (one + two).astype(jnp.bfloat16))
    slot = lax.broadcasted_iota(jnp.int32, (rows, CAP), 1).astype(jnp.float32)
    for i in range(4):
        hit = slot == rank[:, i : i + 1]
        first[i] = jnp.where(hit, one[:, i : i + 1], 0.0).astype(jnp.bfloat16)
        second[i] = jnp.where(hit, two[:, i : i + 1], 0.0).astype(jnp.bfloat16)
    for copy in copies:
        copy.wait()


def slots(routes, down):
    shape = pltpu.VMEM((4, routes.shape[0], CAP), jnp.bfloat16)
    return pl.pallas_call(
        slots_kernel,
        out_shape=(shape, shape, pltpu.VMEM((4, HID, BLK), jnp.bfloat16)),
        in_specs=[VMEM, ANY],
        out_specs=(VMEM,) * 3,
        scratch_shapes=[pltpu.SemaphoreType.DMA((4,))],
        compiler_params=params(4),
    )(routes, distant(down))


def prepare_kernel(own, one, three, two, tokens, gain, first, second, *rest):
    hidden, *outgoing = rest[-5:]
    total = own[...] + tokens[...].astype(jnp.float32)
    for part in (two, one, three):
        total = total + part[...].astype(jnp.float32)
    hidden[...] = total
    x, _, c, _ = position()
    scaled = (total * gain[pl.ds(2 * x + c, 1), :]).astype(jnp.bfloat16)
    for i, out in enumerate(outgoing):
        out[...] = lax.dot_general(
            first[i] + second[i], scaled, (((0,), (0,)), ((), ())), preferred_element_type=jnp.float32
        ).astype(jnp.bfloat16)


def prepare(own, one, three, two, tokens, gain, first, second, swapped):
    rows = tokens.shape[0]
    return pl.pallas_call(
        prepare_kernel,
        out_shape=(pltpu.VMEM((rows, BLK), jnp.float32),)
        + (pltpu.VMEM((CAP, BLK), jnp.bfloat16),) * 4,
        in_specs=[VMEM] * 8 + [ANY] * len(swapped),
        out_specs=(VMEM,) * 5,
        compiler_params=params(4),
        cost_estimate=pl.CostEstimate(
            flops=2 * rows * BLK * 4 * CAP, bytes_accessed=1000000, transcendentals=0
        ),
    )(own, one, three, two, tokens, gain, first, second, *map(distant, swapped))


def join_kernel(a, b, c, d, token, out):
    for i, part in enumerate((a, b, c, d)):
        out[i * ROWS : (i + 1) * ROWS, :] = part[...]


def join(parts):
    token = swap_cores(sum(part[:16, :128].astype(jnp.float32) for part in parts[1:]))
    return pl.pallas_call(
        join_kernel,
        out_shape=pltpu.VMEM((4 * ROWS, BLK), jnp.bfloat16),
        in_specs=[VMEM] * 4 + [ANY],
        out_specs=VMEM,
        compiler_params=params(4),
        cost_estimate=pl.CostEstimate(flops=0, bytes_accessed=2000000, transcendentals=0),
    )(*parts, token)


def line_rows(index):
    return pl.ds(pl.multiple_of(index * ROWS, ROWS), ROWS)


def lanes(value):
    total = value[:, :128]
    for i in range(1, BLK // 128):
        total += value[:, i * 128 : (i + 1) * 128]
    return total


def partner(position, shift):
    return position ^ shift


def walk(held, emit):
    x, y, c, _ = position()
    blocks = [2 * partner(x, shift) + c for shift in OFFS]

    for core in range(2):

        @pl.when(c == core)
        def _(core=core):
            for m, shift in enumerate(OFFS):
                if core == 0:
                    spots = {n: (held.index(m), n) for n in range(4)} if m in held else {}
                else:
                    spots = {n: (j, m) for j, n in enumerate(held)}
                emit(core, line_rows(partner(y, shift)), m, blocks, spots)


def stage_kernel(gate_far, up_far, gate, up, down, down_far, weights, downs, sems):
    x, _, c, _ = position()
    copies = []
    for n, shift in enumerate(OFFS):
        rows = pl.ds(pl.multiple_of((2 * partner(x, shift) + c) * BLK, BLK), BLK)
        columns = pl.ds(pl.multiple_of((2 * partner(x, shift) + c) * BLK, BLK), BLK)
        for which, source in enumerate((gate_far, up_far, gate, up)):
            copies.append((source.at[rows, :], weights.at[which, n]))
        copies.append((down.at[:, columns], downs.at[0, n]))
        copies.append((down_far.at[partner(x, shift)], downs.at[1, n]))
    copies = [pltpu.make_async_copy(*ends, sems.at[i]) for i, ends in enumerate(copies)]
    for copy in copies:
        copy.start()
    for copy in copies:
        copy.wait()


def stage(*sources):
    return pl.pallas_call(
        stage_kernel,
        out_shape=(
            pltpu.VMEM((4, 4, BLK, HID), jnp.bfloat16),
            pltpu.VMEM((2, 4, HID, BLK), jnp.bfloat16),
        ),
        in_specs=[ANY] * 6,
        out_specs=(VMEM, VMEM),
        scratch_shapes=[pltpu.SemaphoreType.DMA((24,))],
        compiler_params=params(12),
        cost_estimate=pl.CostEstimate(flops=0, bytes_accessed=18000000, transcendentals=0),
    )(*map(distant, sources))


def enter_terms(pieces, weights, inverse, route, blocks, spots, which=range(4)):
    def found(n):
        j, i = spots[n]
        return pieces[j, i * ROWS : (i + 1) * ROWS, :]

    def total(terms):
        return functools.reduce(lambda a, b: a + b, terms)

    sums = [total([dot(found(n), weights[w, n]) for n in spots]) for w in which]
    if inverse is None:
        return sums, ()
    squares, products = [], []
    for n in spots:
        value = found(n).astype(jnp.float32)
        plain = value * inverse[pl.ds(blocks[n], 1), :]
        squares.append(lanes(plain * plain))
        products.append(lanes(value * route[pl.ds(blocks[n], 1), :]))
    return sums, (total(squares), total(products))


def put(ref, rows, values):
    start = 0
    for value in values:
        ref[rows, start : start + value.shape[1]] = value.astype(ref.dtype)
        start += value.shape[1]


def enter_first_kernel(p0, p1, weights, inverse, route, own, sums, far, pieces, sems):
    copies = [pltpu.make_async_copy(p, pieces.at[j], sems.at[j]) for j, p in enumerate((p0, p1))]
    for copy in copies:
        copy.start()
    for copy in copies:
        copy.wait()

    def emit(core, rows, m, blocks, spots):
        if spots:
            terms, both = enter_terms(pieces, weights, inverse, route, blocks, spots)
            put(far, rows, terms[:2])
            put(own, rows, terms[2:])
            put(sums, rows, both)

    walk((0, 3), emit)


def enter_second(given, pieces, sems, emit_terms):
    def copies(core, step):
        parts = []
        for j in range(2):
            if core == 0 and j == step or core == 1:
                rows = pl.ds(0, 4 * ROWS) if core == 0 else pl.ds(step * ROWS, ROWS)
                parts.append(
                    pltpu.make_async_copy(given[j].at[rows, :], pieces.at[j, rows, :], sems.at[4 * j + step])
                )
        return parts

    def start(core, step):
        for copy in copies(core, step):
            copy.start()

    def wait(core, step):
        for copy in copies(core, step):
            copy.wait()

    def emit(core, rows, m, blocks, spots):
        if m == 0:
            start(core, 0)
            start(core, 1)
        if core == 0 and m in (1, 2):
            wait(core, m - 1)
        if core == 1:
            wait(core, m)
            if m < 2:
                start(core, m + 2)
        emit_terms(core, rows, blocks, spots)

    walk((1, 2), emit)


def enter_far_kernel(p0, p1, weights, inverse, route, far_first, sums_first, far, sums, pieces, sems):
    def emit(core, rows, blocks, spots):
        far_all, both = far_first[rows, :], sums_first[rows, :]
        if spots:
            terms, more = enter_terms(pieces, weights, inverse, route, blocks, spots, (0, 1))
            terms, more = jnp.concatenate(terms, axis=1), jnp.concatenate(more, axis=1)
            far_all, both = (terms, more) if core == 0 else (terms + far_all, more + both)
        sums[rows, :] = both
        put(far, rows, (far_all, both))

    enter_second((p0, p1), pieces, sems, emit)


def enter_own_kernel(p0, p1, weights, own_first, own, pieces, sems):
    def emit(core, rows, blocks, spots):
        own_all = own_first[rows, :]
        if spots:
            terms, _ = enter_terms(pieces, weights, None, None, blocks, spots, (2, 3))
            terms = jnp.concatenate(terms, axis=1)
            own_all = terms if core == 0 else terms + own_all
        own[rows, :] = own_all

    enter_second((p0, p1), pieces, sems, emit)


def enter(pieces, weights, inverse, route):
    own = pltpu.VMEM((4 * ROWS, 2 * HID), jnp.float32)
    sums = pltpu.VMEM((4 * ROWS, 256), jnp.float32)
    cost = pl.CostEstimate(
        flops=2 * 4 * ROWS * 2 * BLK * 4 * HID, bytes_accessed=5000000, transcendentals=0
    )
    scratch = [pltpu.VMEM((2, 4 * ROWS, BLK), jnp.bfloat16), pltpu.SemaphoreType.DMA((8,))]
    fixed = (near(weights), near(inverse), near(route))
    first = pl.pallas_call(
        enter_first_kernel,
        out_shape=(own, sums, own),
        in_specs=[ANY] * 2 + [VMEM] * 3,
        out_specs=(VMEM,) * 3,
        scratch_shapes=scratch,
        compiler_params=params(10),
        cost_estimate=cost,
    )(distant(pieces[0]), distant(pieces[3]), *fixed)
    own_first, sums_first, far_first = map(near, first)
    given = distant(pieces[1]), distant(pieces[2])
    far, sums = pl.pallas_call(
        enter_far_kernel,
        out_shape=(pltpu.VMEM((4 * ROWS, 2 * HID + 256), jnp.bfloat16), sums),
        in_specs=[ANY] * 2 + [VMEM] * 5,
        out_specs=(VMEM,) * 2,
        scratch_shapes=scratch,
        compiler_params=params(10),
        cost_estimate=cost,
    )(*given, *fixed, far_first, sums_first)
    own = pl.pallas_call(
        enter_own_kernel,
        out_shape=own,
        in_specs=[ANY] * 2 + [VMEM] * 2,
        out_specs=VMEM,
        scratch_shapes=scratch,
        compiler_params=params(10),
        cost_estimate=cost,
    )(*given, fixed[0], own_first)
    return own, sums, far


def activate_kernel(own, sums, far, out, logit):
    for r in range(4):
        rows = slice(r * ROWS, (r + 1) * ROWS)
        other = far[rows, :].astype(jnp.float32)
        both = sums[rows, :] + other[:, 2 * HID :]
        mean = jnp.sum(both[:, :128], axis=1, keepdims=True) * (1.0 / D)
        scale = lax.rsqrt(mean + EPS)
        gate = (own[rows, :HID] + other[:, :HID]) * scale
        upper = (own[rows, HID:] + other[:, HID : 2 * HID]) * scale
        out[rows, :] = (gate * (1.0 / (1.0 + jnp.exp(-gate))) * upper).astype(jnp.bfloat16)
        value = jnp.sum(both[:, 128:], axis=1, keepdims=True) * scale
        logit[rows, :] = jnp.broadcast_to(value, (ROWS, 128))


def activate(own, sums, far):
    return pl.pallas_call(
        activate_kernel,
        out_shape=(
            pltpu.VMEM((4 * ROWS, HID), jnp.bfloat16),
            pltpu.VMEM((4 * ROWS, 128), jnp.float32),
        ),
        in_specs=[VMEM] * 3,
        out_specs=(VMEM,) * 2,
        compiler_params=params(6),
    )(near(own), near(sums), near(far))


def leave_kernel(wanted, act, act_far, downs, *outs):
    _, y, c, _ = position()

    for core in range(2):

        @pl.when(c == core)
        def _(core=core):
            for out, (second, firsts) in zip(outs, wanted):
                for i, first in enumerate(firsts):
                    on_x, on_y = (first, second) if core == 0 else (second, first)
                    rows, n = line_rows(partner(y, on_y)), OFFS.index(on_x)
                    value = dot(act[rows, :], downs[0, n]) + dot(act_far[rows, :], downs[1, n])
                    out[i * ROWS : (i + 1) * ROWS, :] = value.astype(jnp.bfloat16)


def leave(wanted, act, act_far, downs):
    count = sum(len(firsts) for _, firsts in wanted)
    return pl.pallas_call(
        functools.partial(leave_kernel, wanted),
        out_shape=tuple(
            pltpu.VMEM((len(firsts) * ROWS, BLK), jnp.bfloat16) for _, firsts in wanted
        ),
        in_specs=[VMEM] * 3,
        out_specs=(VMEM,) * len(wanted),
        compiler_params=params(6),
        cost_estimate=pl.CostEstimate(
            flops=2 * ROWS * count * BLK * 2 * HID, bytes_accessed=4000000, transcendentals=0
        ),
    )(near(act), near(act_far), near(downs))


def gather_kernel(own, logit, *rest):
    parts, outs = rest[:-4], rest[-4:]
    y = position()[1]
    total = own[...].astype(jnp.float32)
    for part in parts:
        total = total + part[...].astype(jnp.float32)
    for i, out in enumerate(outs):
        out[:, :BLK] = total[i * CAP : (i + 1) * CAP].astype(jnp.bfloat16)
        value = logit[pl.ds(pl.multiple_of(y * ROWS + i * CAP, CAP), CAP), :]
        high = value.astype(jnp.bfloat16)
        low = (value - high.astype(jnp.float32)).astype(jnp.bfloat16)
        lane = lax.broadcasted_iota(jnp.int32, (CAP, 128), 1)
        out[:, BLK:] = jnp.where(lane < 64, high.astype(jnp.float32), low.astype(jnp.float32)).astype(jnp.bfloat16)


def gather(own, parts, logit):
    return pl.pallas_call(
        gather_kernel,
        out_shape=(pltpu.VMEM((CAP, BLK + 128), jnp.bfloat16),) * 4,
        in_specs=[VMEM] * (2 + len(parts)),
        out_specs=(VMEM,) * 4,
        compiler_params=params(6),
        cost_estimate=pl.CostEstimate(flops=2000000, bytes_accessed=2000000, transcendentals=0),
    )(own, near(logit), *parts)


def finish_kernel(hidden, first, second, b0, b1, b2, b3, out):
    def pick(hits):
        return functools.reduce(
            lambda a, b: a + b, [dot(hits[i], block[...]) for i, block in enumerate((b0, b1, b2, b3))]
        )

    one, two = pick(first), pick(second)

    def logit(rows):
        return rows[:, BLK : BLK + 1] + rows[:, BLK + 64 : BLK + 65]

    weight = 1.0 / (1.0 + jnp.exp(logit(two) - logit(one)))
    mixture = weight * one[:, :BLK] + (1.0 - weight) * two[:, :BLK]
    out[...] = (hidden[...] + mixture).astype(jnp.bfloat16)


def finish(hidden, first, second, blocks):
    return pl.pallas_call(
        finish_kernel,
        out_shape=jax.ShapeDtypeStruct(hidden.shape, jnp.bfloat16),
        in_specs=[VMEM] * 7,
        out_specs=VMEM,
        compiler_params=params(6),
        cost_estimate=pl.CostEstimate(flops=40000000, bytes_accessed=2000000, transcendentals=0),
    )(near(hidden), near(first), near(second), *blocks)


def shards(
    tokens,
    queries,
    new_keys,
    new_values,
    key_cache,
    value_cache,
    lengths,
    routes,
    out_weight,
    norm_gain,
    router,
    gate_weight,
    up_weight,
    down_weight,
):
    z = lax.axis_index("z")

    gate_far, up_far = swap_cores(gate_weight), swap_cores(up_weight)
    gain = norm_gain.astype(jnp.float32).reshape(8, BLK)
    inverse = 1.0 / gain

    for_other, context = attend(
        lengths, queries, new_keys, new_values, key_cache, value_cache, out_weight
    )
    for_own = project(context, out_weight)
    mine, one, three, two, routes = combine(for_own, swap_cores(for_other), routes)
    moved = [along_x(one, 1), along_x(three, 3), along_x(two, 2)]
    first_hits, second_hits, down_half = slots(routes, down_weight)
    down_far = swap_cores(down_half)
    hidden, *outgoing = prepare(
        mine, *moved, tokens, gain, first_hits, second_hits, (gate_far, up_far)
    )
    line = jnp.concatenate(
        [outgoing[0]] + [along_z(rows, shift) for rows, shift in zip(outgoing[1:], OFFS[1:])]
    )
    line = join([line] + [along_first(line, shift) for shift in OFFS[1:]])
    pieces = [line] + [along_second(line, shift) for shift in OFFS[1:]]

    route = lax.dynamic_index_in_dim(router, z, 1, keepdims=False).reshape(8, BLK)
    weights, downs = stage(gate_far, up_far, gate_weight, up_weight, down_weight, down_far)
    own, sums, far = enter(pieces, weights, inverse, route)
    act, logit = activate(own, sums, swap_cores(far))
    operands = (act, swap_cores(act), downs)
    rest = OFFS[1:]
    (far2,) = leave(((2, rest),), *operands)
    far1, far3 = leave(((1, rest), (3, rest)), *operands)
    near2, near1, near3, far0, near0 = leave(
        ((2, (0,)), (1, (0,)), (3, (0,)), (0, rest), (0, (0,))), *operands
    )

    def gathered(own, one, three, two):
        total = own.astype(jnp.float32) + along_second(two, 2).astype(jnp.float32)
        total = total + along_second(one, 1).astype(jnp.float32)
        return total + along_second(three, 3).astype(jnp.float32)

    others = gathered(far0, far1, far3, far2).astype(jnp.bfloat16).reshape(3, ROWS, BLK)
    parts = [along_second(near2, 2), along_second(near1, 1), along_second(near3, 3)]
    parts += [along_first(others[i], shift) for i, shift in enumerate(rest)]
    back = gather(near0, parts, logit)
    blocks = [back[0]] + [along_z(block, shift) for block, shift in zip(back[1:], rest)]
    return finish(hidden, first_hits, second_hits, blocks)


def solution(mesh):
    grid = Mesh(mesh.devices.reshape(4, 4, 4, 2), AXES)
    batch, tp = ("z", "y"), ("x", "c")
    return jax.shard_map(
        shards,
        mesh=grid,
        in_specs=(
            P(batch, tp),
            P(batch, tp, None),
            P(batch, tp, None),
            P(batch, tp, None),
            P(batch, tp, None, None),
            P(batch, tp, None, None),
            P(batch),
            P(batch, None),
            P(tp, None),
            P(),
            P(),
            P(None, (*batch, *tp)),
            P(None, (*batch, *tp)),
            P((*batch, *tp), None),
        ),
        out_specs=P(batch, tp),
        check_vma=False,
    )
```

```python
import functools
import math

import jax
import jax.numpy as jnp
from jax import lax
from jax.experimental import pallas as pl
from jax.experimental.pallas import tpu as pltpu
from jax.sharding import Mesh
from jax.sharding import PartitionSpec as P

CAP = 40
EPS = 1e-05
D = 6144
BLK = 768
ROWS = 160
HID = 256
OFFS = (0, 1, 3, 2)
AXES = ("z", "y", "x", "c")
VMEM = pl.BlockSpec(memory_space=pltpu.VMEM)
ANY = pl.BlockSpec(memory_space=pl.ANY)


def device_index(z, y, x, c):
    return ((z * 4 + y) * 4 + x) * 2 + c


def plane_pairs(first, shift):
    pairs = []
    for z in range(4):
        for y in range(4):
            for x in range(4):
                for c in range(2):
                    if (c == 0) == first:
                        target = device_index(z, y, x ^ shift, c)
                    else:
                        target = device_index(z, y ^ shift, x, c)
                    pairs.append((device_index(z, y, x, c), target))
    return pairs


def along_first(a, shift):
    return lax.ppermute(a, AXES, plane_pairs(True, shift))


def along_second(a, shift):
    return lax.ppermute(a, AXES, plane_pairs(False, shift))


def along_z(a, shift):
    return lax.ppermute(a, "z", [(i, i ^ shift) for i in range(4)])


def along_x(a, shift):
    return lax.ppermute(a, "x", [(i, i ^ shift) for i in range(4)])


def swap_cores(a):
    return lax.ppermute(a, "c", [(0, 1), (1, 0)])


def position():
    return [lax.axis_index(name) for name in ("x", "y", "c", "z")]


def near(a):
    return pltpu.with_memory_space_constraint(a, pltpu.VMEM)


def distant(a):
    return pltpu.with_memory_space_constraint(a, pltpu.HBM)


def params(mebibytes):
    return pltpu.CompilerParams(vmem_limit_bytes=mebibytes * 1024 * 1024)


def dot(a, b):
    return jnp.dot(a, b, preferred_element_type=jnp.float32)


def attend_kernel(
    given_lengths, given_queries, given_keys, given_values, keys, values, weight, far, joined,
    lengths, queries, new_keys, new_values, new_key_rows, new_value_rows, key_here, value_here, weight_here, query_here, score, context, sems,
):
    small = [
        pltpu.make_async_copy(source, target, sems.at[16 + n])
        for n, (source, target) in enumerate(
            (
                (given_queries, queries),
                (given_keys, new_keys),
                (given_values, new_values),
                (given_lengths, lengths),
            )
        )
    ]
    for one in small:
        one.start()
    rows, heads, size = queries.shape[1], queries.shape[0], queries.shape[2]
    chunk, core = rows // 4, position()[2]

    def copy(n):
        if n < 8:
            source, target = (keys, key_here) if n < 4 else (values, value_here)
            part = pl.ds(n % 4 * chunk, chunk)
            return pltpu.make_async_copy(source.at[part], target.at[part], sems.at[n])
        start = pl.multiple_of((2 * (n % 4) + 1 - core) * BLK, BLK)
        return pltpu.make_async_copy(weight.at[:, pl.ds(start, BLK)], weight_here.at[n - 8], sems.at[n])

    started = [0]

    def start(until):
        for n in range(started[0], until):
            copy(n).start()
        started[0] = max(started[0], until)

    start(6)
    for one in small:
        one.wait()
    query_here[heads * rows :, :] = jnp.zeros(((8 - heads) * rows, size), jnp.float32)
    new_key_rows[...] = new_keys[...].astype(jnp.float32)
    new_value_rows[...] = new_values[...].astype(jnp.float32)
    for head in range(heads):
        query_here[head * rows : (head + 1) * rows, :] = queries[head].astype(jnp.float32)

    def row(t):
        return slice(8 * t, 8 * t + 8)

    scale = 1.0 / math.sqrt(size)
    for n in range(4):
        copy(n).wait()
        start((8, 9, 10, 11)[n])
        for t in range(n * chunk, (n + 1) * chunk):
            query = query_here[pl.ds(t, 8, stride=rows), :]
            score[row(t), :] = scale * lax.dot_general(
                query.astype(jnp.bfloat16), key_here[t],
                (((1,), (1,)), ((), ())), preferred_element_type=jnp.float32,
            )
    slot = lax.broadcasted_iota(jnp.int32, (8, score.shape[1]), 1)
    for n in range(4):
        copy(n + 4).wait()
        start(12)
        for t in range(n * chunk, (n + 1) * chunk):
            query = query_here[pl.ds(t, 8, stride=rows), :]
            mine = scale * jnp.sum(query * new_key_rows[t : t + 1, :], axis=1, keepdims=True)
            scores = score[row(t), :]
            valid = slot < lengths[t]
            top = jnp.maximum(jnp.max(jnp.where(valid, scores, -jnp.inf), axis=1, keepdims=True), mine)
            weights = jnp.where(valid, jnp.exp(scores - top), 0.0)
            own_weight = jnp.exp(mine - top)
            total = jnp.sum(weights, axis=1, keepdims=True) + own_weight
            probs = (weights / total).astype(jnp.bfloat16)
            own_prob = (own_weight / total).astype(jnp.bfloat16).astype(jnp.float32)
            context[row(t), :] = dot(probs, value_here[t]) + own_prob * new_value_rows[t : t + 1, :]
    for head in range(heads):
        joined[:, head * size : (head + 1) * size] = context[pl.ds(head, rows, stride=8), :].astype(
            jnp.bfloat16
        )
    for n in range(4):
        copy(8 + n).wait()
        far[n] = dot(joined[...], weight_here[n]).astype(far.dtype)


def attend(lengths, queries, new_keys, new_values, keys, values, out_weight):
    rows, heads, size = queries.shape
    length = keys.shape[2]
    return pl.pallas_call(
        attend_kernel,
        out_shape=(
            pltpu.VMEM((4, rows, BLK), jnp.bfloat16),
            pltpu.VMEM((rows, heads * size), jnp.bfloat16),
        ),
        in_specs=[ANY] * 7,
        out_specs=(VMEM, VMEM),
        scratch_shapes=[
            pltpu.SMEM((rows,), jnp.int32),
            pltpu.VMEM((heads, rows, size), jnp.bfloat16),
            pltpu.VMEM((rows, size), jnp.bfloat16),
            pltpu.VMEM((rows, size), jnp.bfloat16),
            pltpu.VMEM((rows, size), jnp.float32),
            pltpu.VMEM((rows, size), jnp.float32),
            pltpu.VMEM((rows, length, size), jnp.bfloat16),
            pltpu.VMEM((rows, length, size), jnp.bfloat16),
            pltpu.VMEM((4, BLK, BLK), jnp.bfloat16),
            pltpu.VMEM((8 * rows, size), jnp.float32),
            pltpu.VMEM((8 * rows, length), jnp.float32),
            pltpu.VMEM((8 * rows, size), jnp.float32),
            pltpu.SemaphoreType.DMA((20,)),
        ],
        compiler_params=params(20),
        cost_estimate=pl.CostEstimate(
            flops=2 * rows * BLK * BLK * 8, bytes_accessed=14000000, transcendentals=0
        ),
    )(
        distant(lengths),
        distant(queries.transpose(1, 0, 2)),
        distant(new_keys.reshape(rows, size)),
        distant(new_values.reshape(rows, size)),
        distant(keys.reshape(rows, length, size)),
        distant(values.reshape(rows, length, size)),
        distant(out_weight),
    )


def project_kernel(context, weight, own, weight_here, sems):
    core = position()[2]
    copies = []
    for n in range(4):
        start = pl.multiple_of((2 * n + core) * BLK, BLK)
        copies.append(
            pltpu.make_async_copy(weight.at[:, pl.ds(start, BLK)], weight_here.at[n], sems.at[n])
        )
    for copy in copies:
        copy.start()
    for n in range(4):
        copies[n].wait()
        own[n] = dot(context[...], weight_here[n])


def project(context, out_weight):
    rows = context.shape[0]
    return pl.pallas_call(
        project_kernel,
        out_shape=pltpu.VMEM((4, rows, BLK), jnp.float32),
        in_specs=[VMEM, ANY],
        out_specs=VMEM,
        scratch_shapes=[pltpu.VMEM((4, BLK, BLK), jnp.bfloat16), pltpu.SemaphoreType.DMA((4,))],
        compiler_params=params(8),
        cost_estimate=pl.CostEstimate(
            flops=2 * rows * BLK * BLK * 4, bytes_accessed=5000000, transcendentals=0
        ),
    )(near(context), distant(out_weight))


def combine_kernel(own, far, routes, mine, one, three, two, handed):
    handed[...] = routes[...]
    for out, shift in ((mine, 0), (one, 1), (three, 3), (two, 2)):
        block = partner(position()[0], shift)
        out[...] = (own[block] + far[block].astype(jnp.float32)).astype(out.dtype)


def combine(own, far, routes):
    rows = own.shape[1]
    return pl.pallas_call(
        combine_kernel,
        out_shape=(pltpu.VMEM((rows, BLK), jnp.float32),)
        + (pltpu.VMEM((rows, BLK), jnp.bfloat16),) * 3
        + (jax.ShapeDtypeStruct(routes.shape, routes.dtype),),
        in_specs=[VMEM] * 3,
        out_specs=(VMEM,) * 5,
        compiler_params=params(4),
    )(near(own), near(far), routes)


def slots_kernel(routes, down, first, second, down_half, sems):
    c = position()[2]
    copies = []
    for k in range(4):
        start = pl.multiple_of((2 * k + 1 - c) * BLK, BLK)
        copies.append(pltpu.make_async_copy(down.at[:, pl.ds(start, BLK)], down_half.at[k], sems.at[k]))
        copies[k].start()
    rows = routes.shape[0]
    lane = lax.broadcasted_iota(jnp.int32, (rows, 128), 1)
    plane = jnp.full((rows, 128), -1, jnp.int32)
    for i, shift in enumerate(OFFS):
        plane = jnp.where(lane == i, partner(position()[3], shift), plane)
    one = jnp.where(routes[:, 0:1] == plane, 1.0, 0.0)
    two = jnp.where(routes[:, 1:2] == plane, 1.0, 0.0)
    before = lax.broadcasted_iota(jnp.int32, (rows, rows), 1) < lax.broadcasted_iota(
        jnp.int32, (rows, rows), 0
    )
    rank = dot(jnp.where(before, 1.0, 0.0).astype(jnp.bfloat16), (one + two).astype(jnp.bfloat16))
    slot = lax.broadcasted_iota(jnp.int32, (rows, CAP), 1).astype(jnp.float32)
    for i in range(4):
        hit = slot == rank[:, i : i + 1]
        first[i] = jnp.where(hit, one[:, i : i + 1], 0.0).astype(jnp.bfloat16)
        second[i] = jnp.where(hit, two[:, i : i + 1], 0.0).astype(jnp.bfloat16)
    for copy in copies:
        copy.wait()


def slots(routes, down):
    shape = pltpu.VMEM((4, routes.shape[0], CAP), jnp.bfloat16)
    return pl.pallas_call(
        slots_kernel,
        out_shape=(shape, shape, pltpu.VMEM((4, HID, BLK), jnp.bfloat16)),
        in_specs=[VMEM, ANY],
        out_specs=(VMEM,) * 3,
        scratch_shapes=[pltpu.SemaphoreType.DMA((4,))],
        compiler_params=params(4),
    )(routes, distant(down))


def prepare_kernel(own, one, three, two, tokens, gain, first, second, *rest):
    hidden, *outgoing = rest[-5:]
    total = own[...] + tokens[...].astype(jnp.float32)
    for part in (two, one, three):
        total = total + part[...].astype(jnp.float32)
    hidden[...] = total
    x, _, c, _ = position()
    scaled = (total * gain[pl.ds(2 * x + c, 1), :]).astype(jnp.bfloat16)
    for i, out in enumerate(outgoing):
        out[...] = lax.dot_general(
            first[i] + second[i], scaled, (((0,), (0,)), ((), ())), preferred_element_type=jnp.float32
        ).astype(jnp.bfloat16)


def prepare(own, one, three, two, tokens, gain, first, second, swapped):
    rows = tokens.shape[0]
    return pl.pallas_call(
        prepare_kernel,
        out_shape=(pltpu.VMEM((rows, BLK), jnp.float32),)
        + (pltpu.VMEM((CAP, BLK), jnp.bfloat16),) * 4,
        in_specs=[VMEM] * 8 + [ANY] * len(swapped),
        out_specs=(VMEM,) * 5,
        compiler_params=params(4),
        cost_estimate=pl.CostEstimate(
            flops=2 * rows * BLK * 4 * CAP, bytes_accessed=1000000, transcendentals=0
        ),
    )(own, one, three, two, tokens, gain, first, second, *map(distant, swapped))


def join_kernel(a, b, c, d, token, out):
    for i, part in enumerate((a, b, c, d)):
        out[i * ROWS : (i + 1) * ROWS, :] = part[...]


def join(parts):
    token = swap_cores(sum(part[:16, :128].astype(jnp.float32) for part in parts[1:]))
    return pl.pallas_call(
        join_kernel,
        out_shape=pltpu.VMEM((4 * ROWS, BLK), jnp.bfloat16),
        in_specs=[VMEM] * 4 + [ANY],
        out_specs=VMEM,
        compiler_params=params(4),
        cost_estimate=pl.CostEstimate(flops=0, bytes_accessed=2000000, transcendentals=0),
    )(*parts, token)


def line_rows(index):
    return pl.ds(pl.multiple_of(index * ROWS, ROWS), ROWS)


def lanes(value):
    total = value[:, :128]
    for i in range(1, BLK // 128):
        total += value[:, i * 128 : (i + 1) * 128]
    return total


def partner(position, shift):
    return position ^ shift


def walk(held, emit):
    x, y, c, _ = position()
    blocks = [2 * partner(x, shift) + c for shift in OFFS]

    for core in range(2):

        @pl.when(c == core)
        def _(core=core):
            for m, shift in enumerate(OFFS):
                if core == 0:
                    spots = {n: (held.index(m), n) for n in range(4)} if m in held else {}
                else:
                    spots = {n: (j, m) for j, n in enumerate(held)}
                emit(core, line_rows(partner(y, shift)), m, blocks, spots)


def stage_kernel(gate_far, up_far, gate, up, down, down_far, weights, downs, sems):
    x, _, c, _ = position()
    copies = []
    for n, shift in enumerate(OFFS):
        rows = pl.ds(pl.multiple_of((2 * partner(x, shift) + c) * BLK, BLK), BLK)
        columns = pl.ds(pl.multiple_of((2 * partner(x, shift) + c) * BLK, BLK), BLK)
        for which, source in enumerate((gate_far, up_far, gate, up)):
            copies.append((source.at[rows, :], weights.at[which, n]))
        copies.append((down.at[:, columns], downs.at[0, n]))
        copies.append((down_far.at[partner(x, shift)], downs.at[1, n]))
    copies = [pltpu.make_async_copy(*ends, sems.at[i]) for i, ends in enumerate(copies)]
    for copy in copies:
        copy.start()
    for copy in copies:
        copy.wait()


def stage(*sources):
    return pl.pallas_call(
        stage_kernel,
        out_shape=(
            pltpu.VMEM((4, 4, BLK, HID), jnp.bfloat16),
            pltpu.VMEM((2, 4, HID, BLK), jnp.bfloat16),
        ),
        in_specs=[ANY] * 6,
        out_specs=(VMEM, VMEM),
        scratch_shapes=[pltpu.SemaphoreType.DMA((24,))],
        compiler_params=params(12),
        cost_estimate=pl.CostEstimate(flops=0, bytes_accessed=18000000, transcendentals=0),
    )(*map(distant, sources))


def enter_terms(pieces, weights, inverse, route, blocks, spots, which=range(4)):
    def found(n):
        j, i = spots[n]
        return pieces[j, i * ROWS : (i + 1) * ROWS, :]

    def total(terms):
        return functools.reduce(lambda a, b: a + b, terms)

    sums = [total([dot(found(n), weights[w, n]) for n in spots]) for w in which]
    if inverse is None:
        return sums, ()
    squares, products = [], []
    for n in spots:
        value = found(n).astype(jnp.float32)
        plain = value * inverse[pl.ds(blocks[n], 1), :]
        squares.append(lanes(plain * plain))
        products.append(lanes(value * route[pl.ds(blocks[n], 1), :]))
    return sums, (total(squares), total(products))


def put(ref, rows, values):
    start = 0
    for value in values:
        ref[rows, start : start + value.shape[1]] = value.astype(ref.dtype)
        start += value.shape[1]


def enter_first_kernel(p0, p1, weights, inverse, route, own, sums, far, pieces, sems):
    copies = [pltpu.make_async_copy(p, pieces.at[j], sems.at[j]) for j, p in enumerate((p0, p1))]
    for copy in copies:
        copy.start()
    for copy in copies:
        copy.wait()

    def emit(core, rows, m, blocks, spots):
        if spots:
            terms, both = enter_terms(pieces, weights, inverse, route, blocks, spots)
            put(far, rows, terms[:2])
            put(own, rows, terms[2:])
            put(sums, rows, both)

    walk((0, 3), emit)


def enter_second(given, pieces, sems, emit_terms):
    def copies(core, step):
        parts = []
        for j in range(2):
            if core == 0 and j == step or core == 1:
                rows = pl.ds(0, 4 * ROWS) if core == 0 else pl.ds(step * ROWS, ROWS)
                parts.append(
                    pltpu.make_async_copy(given[j].at[rows, :], pieces.at[j, rows, :], sems.at[4 * j + step])
                )
        return parts

    def start(core, step):
        for copy in copies(core, step):
            copy.start()

    def wait(core, step):
        for copy in copies(core, step):
            copy.wait()

    def emit(core, rows, m, blocks, spots):
        if m == 0:
            start(core, 0)
            start(core, 1)
        if core == 0 and m in (1, 2):
            wait(core, m - 1)
        if core == 1:
            wait(core, m)
            if m < 2:
                start(core, m + 2)
        emit_terms(core, rows, blocks, spots)

    walk((1, 2), emit)


def enter_far_kernel(p0, p1, weights, inverse, route, far_first, sums_first, far, sums, pieces, sems):
    def emit(core, rows, blocks, spots):
        far_all, both = far_first[rows, :], sums_first[rows, :]
        if spots:
            terms, more = enter_terms(pieces, weights, inverse, route, blocks, spots, (0, 1))
            terms, more = jnp.concatenate(terms, axis=1), jnp.concatenate(more, axis=1)
            far_all, both = (terms, more) if core == 0 else (terms + far_all, more + both)
        sums[rows, :] = both
        put(far, rows, (far_all, both))

    enter_second((p0, p1), pieces, sems, emit)


def enter_own_kernel(p0, p1, weights, own_first, own, pieces, sems):
    def emit(core, rows, blocks, spots):
        own_all = own_first[rows, :]
        if spots:
            terms, _ = enter_terms(pieces, weights, None, None, blocks, spots, (2, 3))
            terms = jnp.concatenate(terms, axis=1)
            own_all = terms if core == 0 else terms + own_all
        own[rows, :] = own_all

    enter_second((p0, p1), pieces, sems, emit)


def enter(pieces, weights, inverse, route):
    own = pltpu.VMEM((4 * ROWS, 2 * HID), jnp.float32)
    sums = pltpu.VMEM((4 * ROWS, 256), jnp.float32)
    cost = pl.CostEstimate(
        flops=2 * 4 * ROWS * 2 * BLK * 4 * HID, bytes_accessed=5000000, transcendentals=0
    )
    scratch = [pltpu.VMEM((2, 4 * ROWS, BLK), jnp.bfloat16), pltpu.SemaphoreType.DMA((8,))]
    fixed = (near(weights), near(inverse), near(route))
    first = pl.pallas_call(
        enter_first_kernel,
        out_shape=(own, sums, own),
        in_specs=[ANY] * 2 + [VMEM] * 3,
        out_specs=(VMEM,) * 3,
        scratch_shapes=scratch,
        compiler_params=params(10),
        cost_estimate=cost,
    )(distant(pieces[0]), distant(pieces[3]), *fixed)
    own_first, sums_first, far_first = map(near, first)
    given = distant(pieces[1]), distant(pieces[2])
    far, sums = pl.pallas_call(
        enter_far_kernel,
        out_shape=(pltpu.VMEM((4 * ROWS, 2 * HID + 256), jnp.bfloat16), sums),
        in_specs=[ANY] * 2 + [VMEM] * 5,
        out_specs=(VMEM,) * 2,
        scratch_shapes=scratch,
        compiler_params=params(10),
        cost_estimate=cost,
    )(*given, *fixed, far_first, sums_first)
    own = pl.pallas_call(
        enter_own_kernel,
        out_shape=own,
        in_specs=[ANY] * 2 + [VMEM] * 2,
        out_specs=VMEM,
        scratch_shapes=scratch,
        compiler_params=params(10),
        cost_estimate=cost,
    )(*given, fixed[0], own_first)
    return own, sums, far


def activate_kernel(own, sums, far, out, logit):
    for r in range(4):
        rows = slice(r * ROWS, (r + 1) * ROWS)
        other = far[rows, :].astype(jnp.float32)
        both = sums[rows, :] + other[:, 2 * HID :]
        mean = jnp.sum(both[:, :128], axis=1, keepdims=True) * (1.0 / D)
        scale = lax.rsqrt(mean + EPS)
        gate = (own[rows, :HID] + other[:, :HID]) * scale
        upper = (own[rows, HID:] + other[:, HID : 2 * HID]) * scale
        out[rows, :] = (gate * (1.0 / (1.0 + jnp.exp(-gate))) * upper).astype(jnp.bfloat16)
        value = jnp.sum(both[:, 128:], axis=1, keepdims=True) * scale
        logit[rows, :] = jnp.broadcast_to(value, (ROWS, 128))


def activate(own, sums, far):
    return pl.pallas_call(
        activate_kernel,
        out_shape=(
            pltpu.VMEM((4 * ROWS, HID), jnp.bfloat16),
            pltpu.VMEM((4 * ROWS, 128), jnp.float32),
        ),
        in_specs=[VMEM] * 3,
        out_specs=(VMEM,) * 2,
        compiler_params=params(6),
    )(near(own), near(sums), near(far))


def leave_kernel(wanted, act, act_far, downs, *outs):
    _, y, c, _ = position()

    for core in range(2):

        @pl.when(c == core)
        def _(core=core):
            for out, (second, firsts) in zip(outs, wanted):
                for i, first in enumerate(firsts):
                    on_x, on_y = (first, second) if core == 0 else (second, first)
                    rows, n = line_rows(partner(y, on_y)), OFFS.index(on_x)
                    value = dot(act[rows, :], downs[0, n]) + dot(act_far[rows, :], downs[1, n])
                    out[i * ROWS : (i + 1) * ROWS, :] = value.astype(jnp.bfloat16)


def leave(wanted, act, act_far, downs):
    count = sum(len(firsts) for _, firsts in wanted)
    return pl.pallas_call(
        functools.partial(leave_kernel, wanted),
        out_shape=tuple(
            pltpu.VMEM((len(firsts) * ROWS, BLK), jnp.bfloat16) for _, firsts in wanted
        ),
        in_specs=[VMEM] * 3,
        out_specs=(VMEM,) * len(wanted),
        compiler_params=params(6),
        cost_estimate=pl.CostEstimate(
            flops=2 * ROWS * count * BLK * 2 * HID, bytes_accessed=4000000, transcendentals=0
        ),
    )(near(act), near(act_far), near(downs))


def gather_kernel(own, logit, *rest):
    parts, outs = rest[:-4], rest[-4:]
    y = position()[1]
    total = own[...].astype(jnp.float32)
    for part in parts:
        total = total + part[...].astype(jnp.float32)
    for i, out in enumerate(outs):
        out[:, :BLK] = total[i * CAP : (i + 1) * CAP].astype(jnp.bfloat16)
        value = logit[pl.ds(pl.multiple_of(y * ROWS + i * CAP, CAP), CAP), :]
        high = value.astype(jnp.bfloat16)
        low = (value - high.astype(jnp.float32)).astype(jnp.bfloat16)
        lane = lax.broadcasted_iota(jnp.int32, (CAP, 128), 1)
        out[:, BLK:] = jnp.where(lane < 64, high.astype(jnp.float32), low.astype(jnp.float32)).astype(jnp.bfloat16)


def gather(own, parts, logit):
    return pl.pallas_call(
        gather_kernel,
        out_shape=(pltpu.VMEM((CAP, BLK + 128), jnp.bfloat16),) * 4,
        in_specs=[VMEM] * (2 + len(parts)),
        out_specs=(VMEM,) * 4,
        compiler_params=params(6),
        cost_estimate=pl.CostEstimate(flops=2000000, bytes_accessed=2000000, transcendentals=0),
    )(own, near(logit), *parts)


def finish_kernel(hidden, first, second, b0, b1, b2, b3, out):
    def pick(hits):
        return functools.reduce(
            lambda a, b: a + b, [dot(hits[i], block[...]) for i, block in enumerate((b0, b1, b2, b3))]
        )

    one, two = pick(first), pick(second)

    def logit(rows):
        return rows[:, BLK : BLK + 1] + rows[:, BLK + 64 : BLK + 65]

    weight = 1.0 / (1.0 + jnp.exp(logit(two) - logit(one)))
    mixture = weight * one[:, :BLK] + (1.0 - weight) * two[:, :BLK]
    out[...] = (hidden[...] + mixture).astype(jnp.bfloat16)


def finish(hidden, first, second, blocks):
    return pl.pallas_call(
        finish_kernel,
        out_shape=jax.ShapeDtypeStruct(hidden.shape, jnp.bfloat16),
        in_specs=[VMEM] * 7,
        out_specs=VMEM,
        compiler_params=params(6),
        cost_estimate=pl.CostEstimate(flops=40000000, bytes_accessed=2000000, transcendentals=0),
    )(near(hidden), near(first), near(second), *blocks)


def shards(
    tokens,
    queries,
    new_keys,
    new_values,
    key_cache,
    value_cache,
    lengths,
    routes,
    out_weight,
    norm_gain,
    router,
    gate_weight,
    up_weight,
    down_weight,
):
    z = lax.axis_index("z")

    gate_far, up_far = swap_cores(gate_weight), swap_cores(up_weight)
    gain = norm_gain.astype(jnp.float32).reshape(8, BLK)
    inverse = 1.0 / gain

    for_other, context = attend(
        lengths, queries, new_keys, new_values, key_cache, value_cache, out_weight
    )
    for_own = project(context, out_weight)
    mine, one, three, two, routes = combine(for_own, swap_cores(for_other), routes)
    moved = [along_x(one, 1), along_x(three, 3), along_x(two, 2)]
    first_hits, second_hits, down_half = slots(routes, down_weight)
    down_far = swap_cores(down_half)
    hidden, *outgoing = prepare(
        mine, *moved, tokens, gain, first_hits, second_hits, (gate_far, up_far)
    )
    line = jnp.concatenate(
        [outgoing[0]] + [along_z(rows, shift) for rows, shift in zip(outgoing[1:], OFFS[1:])]
    )
    line = join([line] + [along_first(line, shift) for shift in OFFS[1:]])
    pieces = [line] + [along_second(line, shift) for shift in OFFS[1:]]

    route = lax.dynamic_index_in_dim(router, z, 1, keepdims=False).reshape(8, BLK)
    weights, downs = stage(gate_far, up_far, gate_weight, up_weight, down_weight, down_far)
    own, sums, far = enter(pieces, weights, inverse, route)
    act, logit = activate(own, sums, swap_cores(far))
    operands = (act, swap_cores(act), downs)
    rest = OFFS[1:]
    (far2,) = leave(((2, rest),), *operands)
    far1, far3 = leave(((1, rest), (3, rest)), *operands)
    near2, near1, near3, far0, near0 = leave(
        ((2, (0,)), (1, (0,)), (3, (0,)), (0, rest), (0, (0,))), *operands
    )

    def gathered(own, one, three, two):
        total = own.astype(jnp.float32) + along_second(two, 2).astype(jnp.float32)
        total = total + along_second(one, 1).astype(jnp.float32)
        return total + along_second(three, 3).astype(jnp.float32)

    others = gathered(far0, far1, far3, far2).astype(jnp.bfloat16).reshape(3, ROWS, BLK)
    parts = [along_second(near2, 2), along_second(near1, 1), along_second(near3, 3)]
    parts += [along_first(others[i], shift) for i, shift in enumerate(rest)]
    back = gather(near0, parts, logit)
    blocks = [back[0]] + [along_z(block, shift) for block, shift in zip(back[1:], rest)]
    return finish(hidden, first_hits, second_hits, blocks)


def solution(mesh):
    grid = Mesh(mesh.devices.reshape(4, 4, 4, 2), AXES)
    batch, tp = ("z", "y"), ("x", "c")
    return jax.shard_map(
        shards,
        mesh=grid,
        in_specs=(
            P(batch, tp),
            P(batch, tp, None),
            P(batch, tp, None),
            P(batch, tp, None),
            P(batch, tp, None, None),
            P(batch, tp, None, None),
            P(batch),
            P(batch, None),
            P(tp, None),
            P(),
            P(),
            P(None, (*batch, *tp)),
            P(None, (*batch, *tp)),
            P((*batch, *tp), None),
        ),
        out_specs=P(batch, tp),
        check_vma=False,
    )
```
